32 devices in a mesh: section: 2 (over x), dp: 16 (over z, y, core).
Axes of the slice: x: 2, y: 2, z: 4, core: 2. Of those that a mesh axis runs over, the one named last changes fastest.
Arguments:
- hidden: bfloat16 [2, 2048, 8192], P('section', 'dp'), may hold values from -6 to 6
- gain_table: bfloat16 [10, 8192], replicated, may hold values from 0.099609375 to 1.8984375
- layer_counts: int32 [2], P('section'), may hold values from 1 to 8, 10 in all
- positions: int32 [2, 2048], P('section', 'dp'), may hold values from 0 to 8191, as said below
- queries: bfloat16 [2, 2048, 4096], P('section', 'dp'), may hold values from -35 to 35
- keys: bfloat16 [2, 2048, 512], P('section', 'dp'), may hold values from -10 to 10
- value_weight: bfloat16 [2, 8192, 512], P('section', 'dp'), may hold values from -0.0625 to 0.0625
- out_grad: bfloat16 [2, 2048, 4096], P('section', 'dp'), may hold values from -6 to 6
Outputs:
- query_grad: bfloat16 [2, 2048, 4096], P('section', 'dp')
- key_grad: bfloat16 [2, 2048, 512], P('section', 'dp')
- value_weight_grad: bfloat16 [2, 8192, 512], P('section', 'dp')
- upstream_grad: bfloat16 [2, 2048, 8192], P('section', 'dp')
The draws below stay inside these ranges and needn't reach their ends.
Inputs may be any that keep to these rules, and one draw needn't show every extreme that they name: Within each device's block of 128 tokens the positions rise by 1 to 3 from token to token.
All inputs are finite; a program needn't handle non-finite values. No bound on the sum of `layer_counts` on one device may be relied on, other than what follows from the above.
Results may differ from the reference program's by a relative error of at most 0.02.
Values may be sent and summed in bfloat16 or wider, within the bound.
No kernel may reach another device: no remote copies, remote signals or barrier semaphores. Data moves between devices by JAX's collectives and lax.ppermute only.
A program may use at most 128 MiB of HBM per device.

```python
import math
import jax
import jax.numpy as jnp
import numpy as np
from jax import lax

D = 8192
HQ = 32
HK = 4
HD = 128
TOK_DEV = 128
MOST_LAYERS = 8
MAXPOS = 8192
SECTIONS = 2
TOKENS = 2048
LAYERS = 10


def draw_pair(key):
    base = jax.random.fold_in(key, 11)
    key_keys, key_queries = jax.random.split(base, 2)
    share = HQ // HK
    keys_raw = jnp.clip(jax.random.normal(key_keys, (SECTIONS, TOKENS, HK, HD), jnp.float32), -4.0, 4.0)
    queries_raw = jnp.clip(jax.random.normal(key_queries, (SECTIONS, TOKENS, HK, share, HD), jnp.float32), -4.0, 4.0)
    return (queries_raw.reshape(SECTIONS, TOKENS, HQ * HD), keys_raw.reshape(SECTIONS, TOKENS, HK * HD))


def draw_queries(key, part):
    return draw_pair(key)[0].astype(jnp.bfloat16)


def draw_keys(key, part):
    return draw_pair(key)[1].astype(jnp.bfloat16)


def draw_positions(key, part):
    blocks = TOKENS // TOK_DEV
    key_step, key_start = jax.random.split(jax.random.fold_in(key, 5), 2)
    steps = jax.random.randint(key_step, (SECTIONS, blocks, TOK_DEV), 1, 4, jnp.int32)
    steps = steps.at[:, :, 0].set(0)
    offsets = jnp.cumsum(steps, axis=2).astype(jnp.int32)
    span = offsets[:, :, TOK_DEV - 1]
    room = (MAXPOS - span).astype(jnp.int32)
    drawn = jax.random.randint(key_start, (SECTIONS, blocks), 0, 1048576, jnp.int32)
    starts = (drawn % room).astype(jnp.int32)
    starts = starts.at[0, 0].set(room[0, 0] - 1)
    starts = starts.at[0, blocks - 1].set(0)
    return (starts[:, :, None] + offsets).reshape(SECTIONS, TOKENS).astype(jnp.int32)


def with_spikes(result, key, source, target, blocks, factor):
    owner, partner = [(jnp.arange(result.shape[axis_at]) // (result.shape[axis_at] // blocks)).reshape([-1 if axis == axis_at else 1 for axis in range(result.ndim)]) for axis_at in (source, target)]
    chosen = jax.random.permutation(key, blocks)[partner]
    strong = (owner == chosen) | (owner == (partner + blocks // 2) % blocks)
    return jnp.where(strong, factor * result, result)


def steps_of(own_key, shape, cuts, low, top_value):
    level, own = 1.0, jax.random.fold_in(own_key, 6)
    for dim, shards_of in cuts:
        draws = jnp.exp(jax.random.uniform(jax.random.fold_in(own, dim), (shards_of,), jnp.float32, low / len(cuts), top_value / len(cuts)))
        level = level * jnp.repeat(draws, shape[dim] // shards_of).reshape([-1 if axis == dim else 1 for axis in range(len(shape))])
    return level


def length_profile(number_of, total, limit, skew):
    portions = [(1 << 20) // math.isqrt(grade ** skew) + 1 for grade in range(2, number_of + 1)]
    surplus, counts = total - limit - (number_of - 1), [1] * (number_of - 1)
    while surplus > 0:
        free = [i for i in range(number_of - 1) if counts[i] < limit]
        whole, left = sum([portions[i] for i in free]), surplus
        for i in free:
            addition = min(limit - counts[i], max(1, left * portions[i] // whole), surplus)
            counts[i] = counts[i] + addition
            surplus = surplus - addition
    return np.array([limit] + counts)


def ragged_sizes(own_key, amount, total, most, slope):
    if amount == 2:
        one = jax.random.randint(own_key, (), max(1, total - most), min(most, total - 1) + 1)
        return jnp.stack([one, total - one])
    tallies = jnp.asarray(length_profile(amount, total, most, slope), jnp.int32)
    twos = (amount - 1) // 2
    source_of, taker = tallies[1:1 + 2 * twos:2], tallies[2:2 + 2 * twos:2]
    slack = jnp.minimum(source_of - 1, most - taker)
    shifted = jax.random.randint(jax.random.fold_in(own_key, 1), (twos,), 0, 1 << 20) % (slack + 1)
    tallies = tallies.at[1:1 + 2 * twos:2].set(source_of - shifted).at[2:2 + 2 * twos:2].set(taker + shifted)
    return tallies[jax.random.permutation(jax.random.fold_in(own_key, 2), amount)]


def centred(key, extent, scale, reach, pieces=(), kind=jnp.bfloat16):
    values = scale * jax.random.normal(key, extent, jnp.float32)
    if pieces:
        values = values * steps_of(key, extent, pieces, -0.22, 0.18)
    return jnp.clip(values, -reach, reach).astype(kind)


def bell_draw_with(key, dims, deviation, limit, cuts, heavy, held_as=jnp.bfloat16):
    values = deviation * jax.random.normal(key, dims, jnp.float32)
    if cuts:
        values = values * steps_of(key, dims, cuts, -0.22, 0.18)
    return jnp.clip(with_spikes(values, jax.random.fold_in(key, 3), *heavy), -limit, limit).astype(held_as)


def setup_inputs(seed: int = 0) -> dict:
    key_list = jax.random.split(jax.random.key(seed), 9)
    return {
        "hidden": bell_draw_with(key_list[0], (SECTIONS, TOKENS, D), 1.0, 6.0, ((0, 2), (1, 16)), (1, 2, 16, 2.0)),
        "gain_table": jnp.clip(1.0 + 0.18 * jax.random.normal(key_list[1], (LAYERS, D), jnp.float32), 0.099609375, 1.8984375).astype(jnp.bfloat16),
        "layer_counts": ragged_sizes(key_list[2], SECTIONS, LAYERS, MOST_LAYERS, 2).astype(jnp.int32),
        "positions": draw_positions(jax.random.fold_in(key_list[8], 71), 0),
        "queries": draw_queries(jax.random.fold_in(key_list[8], 71), 0),
        "keys": draw_keys(jax.random.fold_in(key_list[8], 71), 0),
        "value_weight": centred(key_list[6], (SECTIONS, D, HK * HD), D ** -0.5, 0.0625, ((0, 2), (1, 16))),
        "out_grad": centred(key_list[7], (SECTIONS, TOKENS, HQ * HD), 1.0, 6.0, ((0, 2), (1, 16))),
    }


def rope_angles(places, width):
    half = width // 2
    steps = jnp.arange(half, dtype=jnp.float32)
    freq = jnp.exp(steps * (-2.0 * math.log(500000.0) / width))
    angle = places.astype(jnp.float32)[:, None] * freq[None, :]
    return (jnp.cos(angle), jnp.sin(angle))

def rotate(values, cosine, sine, heads, width):
    rows_here = values.shape[0]
    split = values.reshape(rows_here, heads, 2, width // 2)
    first = split[:, :, 0, :]
    second = split[:, :, 1, :]
    cosine = cosine[:, None, :]
    sine = sine[:, None, :]
    turned = jnp.stack([first * cosine - second * sine, first * sine + second * cosine], axis=2)
    return turned.reshape(rows_here, heads * width)

def attend_back(q_rot, k_rot, v_low, d_out, heads, groups, width):
    rows_here = q_rot.shape[0]
    share = heads // groups
    scale = width ** (-0.5)
    q_four = q_rot.astype(jnp.float32).reshape(rows_here, groups, share, width)
    k_three = k_rot.astype(jnp.float32).reshape(rows_here, groups, width)
    v_three = v_low.astype(jnp.float32).reshape(rows_here, groups, width)
    d_four = d_out.astype(jnp.float32).reshape(rows_here, groups, share, width)
    scores = jnp.einsum('tgrd,ugd->grtu', q_four, k_three) * scale
    later = jnp.arange(rows_here)[:, None] >= jnp.arange(rows_here)[None, :]
    scores = jnp.where(later, scores, -1e+30)
    top = lax.optimization_barrier(jnp.max(scores, axis=-1, keepdims=True))
    expo = jnp.exp(scores - top)
    probs = expo / lax.optimization_barrier(jnp.sum(expo, axis=-1, keepdims=True))
    probs_low = lax.optimization_barrier(probs.astype(jnp.bfloat16)).astype(jnp.float32)
    attended = jnp.einsum('grtu,ugd->tgrd', probs_low, v_three)
    delta = lax.optimization_barrier(jnp.sum(d_four * attended, axis=-1))
    delta = jnp.transpose(delta, (1, 2, 0))[..., None]
    d_probs = jnp.einsum('tgrd,ugd->grtu', d_four, v_three)
    d_scores = (probs * (d_probs - delta) * scale).astype(jnp.bfloat16)
    d_scores = lax.optimization_barrier(d_scores).astype(jnp.float32)
    dq_rot = jnp.einsum('grtu,ugd->tgrd', d_scores, k_three).reshape(rows_here, heads * width)
    dk_rot = jnp.einsum('grtu,tgrd->ugd', d_scores, q_four).reshape(rows_here, groups * width)
    d_values = jnp.einsum('grtu,tgrd->ugd', probs_low, d_four).reshape(rows_here, groups * width)
    return (dq_rot, dk_rot, d_values)

def section_terms(hidden, gain, places, queries, keys, weight, out_grad):
    hidden_f = hidden.astype(jnp.float32)
    gain_f = gain.astype(jnp.float32)
    inverse = lax.rsqrt(lax.optimization_barrier(jnp.mean(hidden_f * hidden_f, axis=-1, keepdims=True)) + 1e-05)
    normed = (hidden_f * inverse * gain_f).astype(jnp.bfloat16)
    values = jnp.dot(normed, weight, preferred_element_type=jnp.float32).astype(jnp.bfloat16)

    def one_sequence(block):
        place_b, query_b, key_b, value_b, grad_b = block
        cosine, sine = rope_angles(place_b, HD)
        q_rot = rotate(query_b.astype(jnp.float32), cosine, sine, HQ, HD).astype(jnp.bfloat16)
        k_rot = rotate(key_b.astype(jnp.float32), cosine, sine, HK, HD).astype(jnp.bfloat16)
        dq_rot, dk_rot, d_values = attend_back(q_rot, k_rot, value_b, grad_b, HQ, HK, HD)
        query_grad = rotate(dq_rot, cosine, -sine, HQ, HD).astype(jnp.bfloat16)
        key_grad = rotate(dk_rot, cosine, -sine, HK, HD).astype(jnp.bfloat16)
        return (query_grad, key_grad, d_values.astype(jnp.bfloat16))
    seqs_here = hidden.shape[0] // TOK_DEV
    blocks = (places.reshape(seqs_here, TOK_DEV), queries.reshape(seqs_here, TOK_DEV, HQ * HD), keys.reshape(seqs_here, TOK_DEV, HK * HD), values.reshape(seqs_here, TOK_DEV, HK * HD), out_grad.reshape(seqs_here, TOK_DEV, HQ * HD))
    query_grad, key_grad, values_grad = lax.map(one_sequence, blocks)
    query_grad = query_grad.reshape(-1, HQ * HD)
    key_grad = key_grad.reshape(-1, HK * HD)
    values_grad = values_grad.reshape(-1, HK * HD)
    weight_grad = jnp.dot(normed.T, values_grad, preferred_element_type=jnp.float32).astype(jnp.bfloat16)
    d_normed = jnp.dot(values_grad, weight.T, preferred_element_type=jnp.float32)
    scaled = gain_f * d_normed
    local_grad = inverse * scaled - hidden_f * inverse ** 3 * lax.optimization_barrier(jnp.mean(hidden_f * scaled, axis=-1, keepdims=True))
    return (query_grad, key_grad, weight_grad, local_grad.astype(jnp.bfloat16))

def reference(hidden, gain_table, layer_counts, positions, queries, keys, value_weight, out_grad):
    last = (jnp.cumsum(layer_counts) - 1).astype(jnp.int32)
    gains = jnp.take(gain_table, last, axis=0)

    def one_section(block):
        return section_terms(*block)
    query_grad, key_grad, weight_grad, local_grad = lax.map(one_section, (hidden, gains, positions, queries, keys, value_weight, out_grad))
    upstream = jnp.concatenate([local_grad[1:], jnp.zeros_like(local_grad[:1])], axis=0)
    return (query_grad, key_grad, weight_grad, upstream)
```

```python
import functools
import math

import jax
import jax.numpy as jnp
from jax import lax
from jax.experimental import pallas as pl
from jax.experimental.pallas import tpu as pltpu
from jax.sharding import PartitionSpec as P

HQ = 32
HK = 4
HD = 128
SHARE = HQ // HK
EPS = 1e-05
F32 = jnp.float32
BF16 = jnp.bfloat16
VMEM_LIMIT = 48 * 1024 * 1024


def params(**more):
    return pltpu.CompilerParams(vmem_limit_bytes=VMEM_LIMIT, **more)


def mm(a, b, contract):
    return lax.dot_general(a, b, ((contract[:1], contract[1:]), ((), ())), preferred_element_type=F32)


def sds(shape, dtype):
    return jax.ShapeDtypeStruct(shape, dtype)


def rope_tables(places):
    half = HD // 2
    steps = jnp.arange(half, dtype=F32)
    freq = jnp.exp(steps * (-2.0 * math.log(500000.0) / HD))
    angle = places.astype(F32)[:, None] * freq[None, :]
    cosine, sine = jnp.cos(angle), jnp.sin(angle)
    return jnp.concatenate([cosine, cosine], 1), jnp.concatenate([-sine, sine], 1)


def turn(x, cosine, sine):
    return x * cosine + pltpu.roll(x, HD // 2, 1) * sine


def turn_back(x, cosine, sine):
    return x * cosine - pltpu.roll(x, HD // 2, 1) * sine


def prep_kernel(where, mine_in, theirs_in, gain_m, gain_t, mine, theirs, gain_out, inverse, total, *, width):
    step = pl.program_id(0)
    rows = lax.broadcasted_iota(jnp.int32, gain_m.shape, 0) == where[0]
    g_m = jnp.sum(jnp.where(rows, gain_m[...].astype(F32), 0.0), axis=0, keepdims=True)
    g_t = jnp.sum(jnp.where(rows, gain_t[...].astype(F32), 0.0), axis=0, keepdims=True)
    h_m = mine_in[...].astype(F32)
    h_t = theirs_in[...].astype(F32)
    mine[0] = (h_m * g_m).astype(BF16)
    theirs[0] = (h_t * g_t).astype(BF16)
    gain_out[0] = g_m
    part = jnp.sum(h_m * h_m + h_t * h_t, axis=1, keepdims=True)

    @pl.when(step == 0)
    def _():
        total[...] = jnp.broadcast_to(part, total.shape)

    @pl.when(step > 0)
    def _():
        total[...] += jnp.broadcast_to(part, total.shape)

    @pl.when(step == pl.num_programs(0) - 1)
    def _():
        inverse[...] = lax.rsqrt(total[...] / width + EPS)


def prep(where, hidden, gain_table, chips, rows):
    tokens, width = hidden.shape
    layers = gain_table.shape[0]
    mine = lambda r, where: (0, where[1 + r])
    theirs = lambda r, where: (0, where[1 + chips + r])
    return pl.pallas_call(
        functools.partial(prep_kernel, width=width),
        grid_spec=pltpu.PrefetchScalarGridSpec(
            num_scalar_prefetch=1,
            grid=(chips,),
            in_specs=[
                pl.BlockSpec((tokens, rows), mine),
                pl.BlockSpec((tokens, rows), theirs),
                pl.BlockSpec((layers, rows), mine),
                pl.BlockSpec((layers, rows), theirs),
            ],
            out_specs=[
                pl.BlockSpec((1, tokens, rows), lambda r, where: (r, 0, 0)),
                pl.BlockSpec((1, tokens, rows), lambda r, where: (r, 0, 0)),
                pl.BlockSpec((1, 1, rows), lambda r, where: (r, 0, 0)),
                pl.BlockSpec((tokens, HD), lambda r, where: (0, 0)),
            ],
            scratch_shapes=[pltpu.VMEM((tokens, HD), F32)],
        ),
        out_shape=[
            sds((chips, tokens, rows), BF16),
            sds((chips, tokens, rows), BF16),
            sds((chips, 1, rows), F32),
            sds((tokens, HD), F32),
        ],
        compiler_params=params(),
        name="prep",
    )(where, hidden, hidden, gain_table, gain_table)


def stacked(ref):
    return jnp.concatenate([ref[:, h * HD : (h + 1) * HD] for h in range(SHARE)], axis=0)


def probs_kernel(q_ref, k_ref, d_ref, cosine, sine, inverse, probs, q_out, k_out, vgs):
    cos, sin = cosine[...], sine[...]
    tokens = k_ref.shape[0]
    k_rot = turn(k_ref[...].astype(F32), cos, sin).astype(BF16)
    q_rot = jnp.concatenate(
        [turn(q_ref[:, h * HD : (h + 1) * HD].astype(F32), cos, sin).astype(BF16) for h in range(SHARE)],
        axis=0,
    )
    q_out[0] = q_rot
    k_out[0] = k_rot
    scores = mm(k_rot, q_rot, (1, 1)) * (HD**-0.5)
    key_at = lax.broadcasted_iota(jnp.int32, (tokens, tokens), 0)
    query_at = lax.broadcasted_iota(jnp.int32, (tokens, tokens), 1)
    seen = key_at <= query_at
    lows = []
    for h in range(SHARE):
        s = jnp.where(seen, scores[:, h * tokens : (h + 1) * tokens], -1e30)
        e = jnp.exp(s - jnp.max(s, axis=0, keepdims=True))
        p = e / jnp.sum(e, axis=0, keepdims=True)
        probs[0, :, h * tokens : (h + 1) * tokens] = p
        lows.append(p.astype(BF16))
    grad = mm(jnp.concatenate(lows, axis=1), stacked(d_ref), (1, 0))
    vgs[...] = (grad * inverse[...]).astype(BF16)


def attention_probs(queries, keys, out_grad, cosine, sine, inverse):
    tokens = queries.shape[0]
    group = pl.BlockSpec((tokens, SHARE * HD), lambda g: (0, g))
    head = pl.BlockSpec((tokens, HD), lambda g: (0, g))
    table = pl.BlockSpec((tokens, HD), lambda g: (0, 0))
    return pl.pallas_call(
        probs_kernel,
        grid=(HK,),
        in_specs=[group, head, group, table, table, table],
        out_specs=[
            pl.BlockSpec((1, tokens, SHARE * tokens), lambda g: (g, 0, 0)),
            pl.BlockSpec((1, SHARE * tokens, HD), lambda g: (g, 0, 0)),
            pl.BlockSpec((1, tokens, HD), lambda g: (g, 0, 0)),
            head,
        ],
        out_shape=[
            sds((HK, tokens, SHARE * tokens), F32),
            sds((HK, SHARE * tokens, HD), BF16),
            sds((HK, tokens, HD), BF16),
            sds((tokens, HK * HD), BF16),
        ],
        compiler_params=params(),
        name="probs",
    )(queries, keys, out_grad, cosine, sine, inverse)


def back_kernel(probs, q_rot, k_rot, d_ref, u_one, u_two, cosine, sine, inverse, dq, dk):
    cos, sin = cosine[...], sine[...]
    tokens = k_rot.shape[1]
    values = ((u_one[...] + u_two[...]) * inverse[...]).astype(BF16)
    d_probs = mm(values, stacked(d_ref), (1, 1))
    p = probs[0]
    delta = jnp.sum(p.astype(BF16).astype(F32) * d_probs, axis=0, keepdims=True)
    d_scores = (p * (d_probs - delta) * (HD**-0.5)).astype(BF16)
    dk[...] = turn_back(mm(d_scores, q_rot[0], (1, 0)), cos, sin).astype(BF16)
    key = k_rot[0]
    for h in range(SHARE):
        part = mm(d_scores[:, h * tokens : (h + 1) * tokens], key, (0, 0))
        dq[:, h * HD : (h + 1) * HD] = turn_back(part, cos, sin).astype(BF16)


def attention_back(probs, q_rot, k_rot, out_grad, u_one, u_two, cosine, sine, inverse):
    tokens = out_grad.shape[0]
    group = pl.BlockSpec((tokens, SHARE * HD), lambda g: (0, g))
    head = pl.BlockSpec((tokens, HD), lambda g: (0, g))
    table = pl.BlockSpec((tokens, HD), lambda g: (0, 0))
    return pl.pallas_call(
        back_kernel,
        grid=(HK,),
        in_specs=[
            pl.BlockSpec((1, tokens, SHARE * tokens), lambda g: (g, 0, 0)),
            pl.BlockSpec((1, SHARE * tokens, HD), lambda g: (g, 0, 0)),
            pl.BlockSpec((1, tokens, HD), lambda g: (g, 0, 0)),
            group,
            head,
            head,
            table,
            table,
            table,
        ],
        out_specs=[group, head],
        out_shape=[sds((tokens, HQ * HD), BF16), sds((tokens, HK * HD), BF16)],
        compiler_params=params(),
        name="back",
    )(probs, q_rot, k_rot, out_grad, u_one, u_two, cosine, sine, inverse)


def values_kernel(*refs, blocks, last):
    mine, theirs = refs[0], refs[1]
    weights = refs[2 : 2 + len(blocks)]
    rest = refs[2 + len(blocks) :]
    tokens = mine.shape[1]
    acc = None
    for r, w in zip(blocks, weights, strict=True):
        left = jnp.concatenate([mine[r], theirs[r]], axis=0)
        part = mm(left, w[...], (1, 0))
        acc = part if acc is None else acc + part
    if not last:
        rest[0][...] = acc
        return
    before, vgs_m, vgs_t, u_mine, u_theirs, dots = rest
    acc = acc + before[...]
    u_mine[...] = acc[:tokens]
    u_theirs[...] = acc[tokens:]
    dot_m = jnp.sum(acc[:tokens] * vgs_m[...].astype(F32), axis=1, keepdims=True)
    dot_t = jnp.sum(acc[tokens:] * vgs_t[...].astype(F32), axis=1, keepdims=True)
    dots[:tokens, :] = jnp.broadcast_to(dot_m, (tokens, HD))
    dots[tokens:, :] = jnp.broadcast_to(dot_t, (tokens, HD))


def values_some(mine, theirs, blocks, weights):
    tokens, wide = mine.shape[1], weights[0].shape[1]
    return pl.pallas_call(
        functools.partial(values_kernel, blocks=blocks, last=False),
        out_shape=sds((2 * tokens, wide), F32),
        compiler_params=params(),
        name="values_some",
    )(mine, theirs, *weights)


def values_last(mine, theirs, blocks, weights, before, vgs_m, vgs_t):
    tokens, wide = mine.shape[1], weights[0].shape[1]
    return pl.pallas_call(
        functools.partial(values_kernel, blocks=blocks, last=True),
        out_shape=[sds((tokens, wide), F32), sds((tokens, wide), F32), sds((2 * tokens, HD), F32)],
        compiler_params=params(),
        name="values_last",
    )(mine, theirs, *weights, before, vgs_m, vgs_t)


def local_kernel(*refs, blocks, width):
    (mine, theirs, vgs_m, vgs_t, gain, inv_m, inv_t, own, got) = refs[:9]
    weights = refs[9 : 9 + len(blocks)]
    out_m, out_t = refs[9 + len(blocks) :]
    tokens, rows = mine.shape[1:]
    c_m = inv_m[...] * inv_m[...] * (own[:tokens, :] + got[tokens:, :]) / width
    c_t = inv_t[...] * inv_t[...] * (own[tokens:, :] + got[:tokens, :]) / width
    c_m = jnp.concatenate([c_m] * (rows // HD), axis=1)
    c_t = jnp.concatenate([c_t] * (rows // HD), axis=1)
    left = jnp.concatenate([vgs_m[...], vgs_t[...]], axis=0)
    for i, (r, w) in enumerate(zip(blocks, weights, strict=True)):
        g = gain[r]
        over = 1.0 / g
        part = mm(left, w[...], (1, 1))
        out_m[:, i * rows : (i + 1) * rows] = (part[:tokens] * g - mine[r].astype(F32) * over * c_m).astype(BF16)
        out_t[:, i * rows : (i + 1) * rows] = (part[tokens:] * g - theirs[r].astype(F32) * over * c_t).astype(BF16)


def local_grads(mine, theirs, vgs_m, vgs_t, gain, inv_m, inv_t, own, got, blocks, weights, width):
    tokens, rows = mine.shape[1:]
    out = sds((tokens, len(blocks) * rows), BF16)
    return pl.pallas_call(
        functools.partial(local_kernel, blocks=blocks, width=width),
        out_shape=[out, out],
        compiler_params=params(),
        name="local_grad",
    )(mine, theirs, vgs_m, vgs_t, gain, inv_m, inv_t, own, got, *weights)


def weight_kernel(*refs, ahead, behind, step, steps):
    mine, theirs, vgs_m, vgs_t = refs[:4]
    right = jnp.concatenate([vgs_m[...], vgs_t[...]], axis=0)
    rows = mine.shape[2]
    half = rows // 2

    def part(r):
        return mm(jnp.concatenate([mine[r], theirs[r]], axis=0), right, (0, 0))

    if step == 0:
        both = part(ahead)
        refs[4][...] = both[:half].astype(BF16)
        refs[5][...] = both[half:].astype(BF16)
        return
    from_f, from_b = refs[4][...].astype(F32), refs[5][...].astype(F32)
    if step == steps:
        total = part(0)
        if steps > 1:
            total = total + from_f + from_b
        else:
            total = total + jnp.concatenate([from_f, from_b], axis=0)
        refs[6][...] = total.astype(BF16)
        return
    f, b = part(ahead), part(behind)
    if step == 1:
        f = jnp.concatenate([f[:half] + from_f, f[half:]], axis=0)
        b = jnp.concatenate([b[:half], b[half:] + from_b], axis=0)
    else:
        f, b = f + from_f, b + from_b
    refs[6][...] = f.astype(BF16)
    refs[7][...] = b.astype(BF16)


def weight_step(mine, theirs, vgs_m, vgs_t, arrived, step, steps):
    chips, _, rows = mine.shape
    wide = vgs_m.shape[1]
    if step == 0:
        out = [sds((rows // 2, wide), BF16)] * 2
    elif step == steps:
        out = sds((rows, wide), BF16)
    else:
        out = [sds((rows, wide), BF16)] * 2
    return pl.pallas_call(
        functools.partial(
            weight_kernel, ahead=steps - step, behind=chips - steps + step, step=step, steps=steps
        ),
        out_shape=out,
        compiler_params=params(),
        name="weight_step",
    )(mine, theirs, vgs_m, vgs_t, *arrived)


def join_kernel(where, *refs, blocks, rows):
    pieces, out, sem = refs[:-2], refs[-2], refs[-1]
    copies = []
    chips = sum(len(b) for b in blocks)
    for i, held in enumerate(blocks):
        for side in range(2):
            for j, r in enumerate(held):
                column = pl.multiple_of(where[1 + side * chips + r] * rows, rows)
                copies.append(
                    pltpu.make_async_copy(
                        pieces[2 * i + side].at[:, j * rows : (j + 1) * rows],
                        out.at[:, pl.ds(column, rows)],
                        sem.at[len(copies)],
                    )
                )
    for copy in copies:
        copy.start()
    for copy in copies:
        copy.wait()


def join(where, pieces, blocks, rows, tokens, width):
    return pl.pallas_call(
        functools.partial(join_kernel, blocks=blocks, rows=rows),
        in_specs=[pl.BlockSpec(memory_space=pltpu.SMEM)] + [pl.BlockSpec(memory_space=pl.ANY)] * len(pieces),
        out_specs=pl.BlockSpec(memory_space=pl.ANY),
        out_shape=sds((tokens, width), BF16),
        scratch_shapes=[pltpu.SemaphoreType.DMA((width // rows,))],
        compiler_params=params(),
        name="join",
    )(where, *pieces)


def last_layer(layer_counts, layers):
    sections, mine = lax.axis_size("section"), lax.axis_index("section")
    own = layer_counts[0]
    total = own
    if sections > 2:
        reach = 1
        while reach < sections:
            route = [(i, i + reach) for i in range(sections - reach)]
            total = total + lax.ppermute(total, "section", route)
            reach *= 2
    return jnp.where(mine == sections - 1, layers, total) - 1


def shards(hidden, gain_table, layer_counts, positions, queries, keys, value_weight, out_grad):
    tokens_in, weight = hidden[0], value_weight[0]
    tokens, width = tokens_in.shape
    rows = weight.shape[0]
    sections = lax.axis_size("section")
    devices = lax.axis_size("dp")
    chips = devices // 2
    ring = list(range(0, chips, 2)) + list(range(1, chips, 2))[::-1]
    place_of = [ring.index(c) for c in range(chips)]
    me = lax.axis_index("dp")
    chip, core = me // 2, me % 2
    place = jnp.asarray(place_of, jnp.int32)[chip]
    around = jnp.asarray(ring + ring, jnp.int32)
    order = lax.dynamic_slice(around, (place,), (chips,)) * 2

    def hop(d, by):
        return 2 * ring[(place_of[d // 2] + by) % chips] + d % 2

    forth = [(d, hop(d, 1)) for d in range(devices)]
    back = [(d, hop(d, -1)) for d in range(devices)]
    swap = [(d, d ^ 1) for d in range(devices)]
    down = [(s * devices + d, (s - 1) * devices + d) for s in range(1, sections) for d in range(devices)]
    cross = [(s * devices + d, (s - 1) * devices + (d ^ 1)) for s in range(1, sections) for d in range(devices)]

    last = last_layer(layer_counts, gain_table.shape[0])
    where = jnp.concatenate([last[None], order + core, order + 1 - core]).astype(jnp.int32)
    mine, send, gain, inverse = prep(where, tokens_in, gain_table, chips, rows)
    theirs = lax.ppermute(send, "dp", swap)
    inverse_t = lax.ppermute(inverse, "dp", swap)
    cosine, sine = rope_tables(positions[0])
    probs, q_rot, k_rot, vgs = attention_probs(queries[0], keys[0], out_grad[0], cosine, sine, inverse)
    vgs_t = lax.ppermute(vgs, "dp", swap)

    held = {0: weight}
    half = chips // 2
    f = b = weight
    for step in range(1, half):
        f = lax.ppermute(f, "dp", forth)
        b = lax.ppermute(b, "dp", back)
        held[chips - step] = f
        held[step] = b
    top = lax.ppermute(f[: rows // 2], "dp", forth)
    bottom = lax.ppermute(b[rows // 2 :], "dp", back)
    early = [r for r in range(chips) if r != half]
    part = values_some(mine, theirs, early, [held[r] for r in early])
    held[half] = jnp.concatenate([top, bottom], axis=0)
    u_mine, u_send, dots = values_last(mine, theirs, [half], [held[half]], part, vgs, vgs_t)
    u_got = lax.ppermute(u_send, "dp", swap)
    dots_got = lax.ppermute(dots, "dp", swap)

    pieces, blocks = [], []
    for at in range(0, chips, 2):
        some = [at, at + 1]
        out_m, out_t = local_grads(
            mine, theirs, vgs, vgs_t, gain, inverse, inverse_t, dots, dots_got, some, [held[r] for r in some], width
        )
        pieces += [lax.ppermute(out_m, ("section", "dp"), down), lax.ppermute(out_t, ("section", "dp"), cross)]
        blocks.append(some)
    upstream = join(where, pieces, blocks, rows, tokens, width)

    vgs_ring, _ = lax.optimization_barrier((vgs, dots))
    arrived = []
    for step in range(half):
        f, b = weight_step(mine, theirs, vgs_ring, vgs_t, arrived, step, half)
        arrived = [lax.ppermute(f, "dp", forth), lax.ppermute(b, "dp", back)]
    weight_grad = weight_step(mine, theirs, vgs_ring, vgs_t, arrived, half, half)

    query_grad, key_grad = attention_back(
        probs, q_rot, k_rot, out_grad[0], u_mine, u_got, cosine, sine, inverse
    )
    return (query_grad[None], key_grad[None], weight_grad[None], upstream[None])


def solution(mesh):
    split = P("section", "dp", None)
    in_specs = (split, P(), P("section"), P("section", "dp"), split, split, split, split)
    out_specs = (split,) * 4
    return jax.shard_map(shards, mesh=mesh, in_specs=in_specs, out_specs=out_specs, check_vma=False)
```

```python
import functools
import math

import jax
import jax.numpy as jnp
from jax import lax
from jax.experimental import pallas as pl
from jax.experimental.pallas import tpu as pltpu
from jax.sharding import PartitionSpec as P

HQ = 32
HK = 4
HD = 128
SHARE = HQ // HK
EPS = 1e-05
F32 = jnp.float32
BF16 = jnp.bfloat16
VMEM_LIMIT = 48 * 1024 * 1024


def cost(us):
    return pl.CostEstimate(flops=int(us * 1e9) + 1, bytes_accessed=1024, transcendentals=0)


SMALL = cost(0.2)
STAGE = 3.0
SWAP = 12.0
PACKED = 6.0
RING = 6.0
LITTLE = 1.0


def params(**more):
    return pltpu.CompilerParams(vmem_limit_bytes=VMEM_LIMIT, **more)


def mm(a, b, contract):
    return lax.dot_general(a, b, ((contract[:1], contract[1:]), ((), ())), preferred_element_type=F32)


def sds(shape, dtype):
    return jax.ShapeDtypeStruct(shape, dtype)


def rope_tables(places):
    half = HD // 2
    steps = jnp.arange(half, dtype=F32)
    freq = jnp.exp(steps * (-2.0 * math.log(500000.0) / HD))
    angle = places.astype(F32)[:, None] * freq[None, :]
    cosine, sine = jnp.cos(angle), jnp.sin(angle)
    return jnp.concatenate([cosine, cosine], 1), jnp.concatenate([-sine, sine], 1)


def turn(x, cosine, sine):
    return x * cosine + pltpu.roll(x, HD // 2, 1) * sine


def turn_back(x, cosine, sine):
    return x * cosine - pltpu.roll(x, HD // 2, 1) * sine


def prep_kernel(
    where, mine_in, theirs_in, gain_m, gain_t, mine, theirs, gain_out, inverse, total, *, width
):
    step = pl.program_id(0)
    rows = lax.broadcasted_iota(jnp.int32, gain_m.shape, 0) == where[0]
    g_m = jnp.sum(jnp.where(rows, gain_m[...].astype(F32), 0.0), axis=0, keepdims=True)
    g_t = jnp.sum(jnp.where(rows, gain_t[...].astype(F32), 0.0), axis=0, keepdims=True)
    h_m = mine_in[...].astype(F32)
    h_t = theirs_in[...].astype(F32)
    mine[0] = (h_m * g_m).astype(BF16)
    theirs[0] = (h_t * g_t).astype(BF16)
    gain_out[0] = g_m
    part = jnp.sum(h_m * h_m + h_t * h_t, axis=1, keepdims=True)
    @pl.when(step == 0)
    def _():
        total[...] = jnp.broadcast_to(part, total.shape)

    @pl.when(step > 0)
    def _():
        total[...] += jnp.broadcast_to(part, total.shape)

    @pl.when(step == pl.num_programs(0) - 1)
    def _():
        inverse[...] = lax.rsqrt(total[...] / width + EPS)


def prep(where, hidden, gain_table, chips, rows):
    tokens, width = hidden.shape
    layers = gain_table.shape[0]
    mine = lambda r, where: (0, where[1 + r])
    theirs = lambda r, where: (0, where[1 + chips + r])
    return pl.pallas_call(
        functools.partial(prep_kernel, width=width),
        grid_spec=pltpu.PrefetchScalarGridSpec(
            num_scalar_prefetch=1,
            grid=(chips,),
            in_specs=[
                pl.BlockSpec((tokens, rows), mine),
                pl.BlockSpec((tokens, rows), theirs),
                pl.BlockSpec((layers, rows), mine),
                pl.BlockSpec((layers, rows), theirs),
            ],
            out_specs=[
                pl.BlockSpec((1, tokens, rows), lambda r, where: (r, 0, 0)),
                pl.BlockSpec((1, tokens, rows), lambda r, where: (r, 0, 0)),
                pl.BlockSpec((1, 1, rows), lambda r, where: (r, 0, 0)),
                pl.BlockSpec((tokens, HD), lambda r, where: (0, 0)),
            ],
            scratch_shapes=[pltpu.VMEM((tokens, HD), F32)],
        ),
        out_shape=[
            sds((chips, tokens, rows), BF16),
            sds((chips, tokens, rows), BF16),
            sds((chips, 1, rows), F32),
            sds((tokens, HD), F32),
        ],
        compiler_params=params(),
        cost_estimate=SMALL,
        name="prep",
    )(where, hidden, hidden, gain_table, gain_table)


def pick_kernel(where, hidden, out_m, out_t, sem, *, soon, chips):
    rows = out_m.shape[2]
    copies = []
    for side, out in enumerate((out_m, out_t)):
        for i, r in enumerate(soon):
            column = pl.multiple_of(where[1 + side * chips + r] * rows, rows)
            source = hidden.at[:, pl.ds(column, rows)]
            copies.append(pltpu.make_async_copy(source, out.at[i], sem.at[side, i]))
    for copy in copies:
        copy.start()
    for copy in copies:
        copy.wait()


def pick(where, hidden, soon, chips, rows):
    somewhere = pl.BlockSpec(memory_space=pl.ANY)
    return pl.pallas_call(
        functools.partial(pick_kernel, soon=soon, chips=chips),
        in_specs=[pl.BlockSpec(memory_space=pltpu.SMEM), somewhere],
        out_specs=[somewhere, somewhere],
        out_shape=[sds((len(soon), hidden.shape[0], rows), BF16)] * 2,
        scratch_shapes=[pltpu.SemaphoreType.DMA((2, len(soon)))],
        compiler_params=params(),
        cost_estimate=SMALL,
        name="pick",
    )(where, hidden)


def stacked(ref):
    return jnp.concatenate([ref[:, h * HD : (h + 1) * HD] for h in range(SHARE)], axis=0)


def probs_kernel(q_ref, k_ref, d_ref, cosine, sine, inverse, probs, q_out, k_out, vgs):
    cos, sin = cosine[...], sine[...]
    tokens = k_ref.shape[0]
    k_rot = turn(k_ref[...].astype(F32), cos, sin).astype(BF16)
    q_rot = jnp.concatenate(
        [turn(q_ref[:, h * HD : (h + 1) * HD].astype(F32), cos, sin).astype(BF16) for h in range(SHARE)],
        axis=0,
    )
    q_out[0] = q_rot
    k_out[0] = k_rot
    scores = mm(k_rot, q_rot, (1, 1)) * (HD**-0.5)
    key_at = lax.broadcasted_iota(jnp.int32, (tokens, tokens), 0)
    query_at = lax.broadcasted_iota(jnp.int32, (tokens, tokens), 1)
    seen = key_at <= query_at
    lows = []
    for h in range(SHARE):
        s = jnp.where(seen, scores[:, h * tokens : (h + 1) * tokens], -1e30)
        e = jnp.exp(s - jnp.max(s, axis=0, keepdims=True))
        p = e / jnp.sum(e, axis=0, keepdims=True)
        probs[0, :, h * tokens : (h + 1) * tokens] = p
        lows.append(p.astype(BF16))
    grad = mm(jnp.concatenate(lows, axis=1), stacked(d_ref), (1, 0))
    vgs[...] = (grad * inverse[...]).astype(BF16)


def attention_probs(queries, keys, out_grad, cosine, sine, inverse):
    tokens = queries.shape[0]
    group = pl.BlockSpec((tokens, SHARE * HD), lambda g: (0, g))
    head = pl.BlockSpec((tokens, HD), lambda g: (0, g))
    table = pl.BlockSpec((tokens, HD), lambda g: (0, 0))
    return pl.pallas_call(
        probs_kernel,
        grid=(HK,),
        in_specs=[group, head, group, table, table, table],
        out_specs=[
            pl.BlockSpec((1, tokens, SHARE * tokens), lambda g: (g, 0, 0)),
            pl.BlockSpec((1, SHARE * tokens, HD), lambda g: (g, 0, 0)),
            pl.BlockSpec((1, tokens, HD), lambda g: (g, 0, 0)),
            head,
        ],
        out_shape=[
            sds((HK, tokens, SHARE * tokens), F32),
            sds((HK, SHARE * tokens, HD), BF16),
            sds((HK, tokens, HD), BF16),
            sds((tokens, HK * HD), BF16),
        ],
        compiler_params=params(),
        cost_estimate=SMALL,
        name="probs",
    )(queries, keys, out_grad, cosine, sine, inverse)


def back_kernel(probs, q_rot, k_rot, d_ref, u_one, u_two, cosine, sine, inverse, dq, dk):
    cos, sin = cosine[...], sine[...]
    tokens = k_rot.shape[1]
    values = ((u_one[...] + u_two[...]) * inverse[...]).astype(BF16)
    d_probs = mm(values, stacked(d_ref), (1, 1))
    p = probs[0]
    delta = jnp.sum(p.astype(BF16).astype(F32) * d_probs, axis=0, keepdims=True)
    d_scores = (p * (d_probs - delta) * (HD**-0.5)).astype(BF16)
    dk[...] = turn_back(mm(d_scores, q_rot[0], (1, 0)), cos, sin).astype(BF16)
    key = k_rot[0]
    for h in range(SHARE):
        part = mm(d_scores[:, h * tokens : (h + 1) * tokens], key, (0, 0))
        dq[:, h * HD : (h + 1) * HD] = turn_back(part, cos, sin).astype(BF16)


def attention_back(probs, q_rot, k_rot, out_grad, u_one, u_two, cosine, sine, inverse):
    tokens = out_grad.shape[0]
    group = pl.BlockSpec((tokens, SHARE * HD), lambda g: (0, g))
    head = pl.BlockSpec((tokens, HD), lambda g: (0, g))
    table = pl.BlockSpec((tokens, HD), lambda g: (0, 0))
    return pl.pallas_call(
        back_kernel,
        grid=(HK,),
        in_specs=[
            pl.BlockSpec((1, tokens, SHARE * tokens), lambda g: (g, 0, 0)),
            pl.BlockSpec((1, SHARE * tokens, HD), lambda g: (g, 0, 0)),
            pl.BlockSpec((1, tokens, HD), lambda g: (g, 0, 0)),
            group,
            head,
            head,
            table,
            table,
            table,
        ],
        out_specs=[group, head],
        out_shape=[sds((tokens, HQ * HD), BF16), sds((tokens, HK * HD), BF16)],
        compiler_params=params(),
        cost_estimate=SMALL,
        name="back",
    )(probs, q_rot, k_rot, out_grad, u_one, u_two, cosine, sine, inverse)


def span(part, rows):
    side = part[1]
    return slice(0, rows) if side is None else slice(side * rows // 2, (side + 1) * rows // 2)


def features(ref, part):
    return ref[part[0]][:, span(part, ref.shape[2])]


def both_vgs(vgs, vgs_t):
    return jnp.concatenate([vgs[...], vgs_t[...]], axis=0)


def pair(mine, theirs, part):
    return jnp.concatenate([features(mine, part), features(theirs, part)], axis=0)


def values_kernel(*refs, parts, first, last):
    mine, theirs = refs[0], refs[1]
    weights, rest = refs[2 : 2 + len(parts)], refs[2 + len(parts) :]
    tokens = mine.shape[1]
    acc = None
    if not first:
        acc, rest = rest[0][...], rest[1:]
    for part, w in zip(parts, weights, strict=True):
        product = mm(pair(mine, theirs, part), w[...], (1, 0))
        acc = product if acc is None else acc + product
    if not last:
        rest[0][...] = acc
        return
    vgs, vgs_t, inverse, u_mine, packed = rest
    vgs = both_vgs(vgs, vgs_t).astype(F32)
    wide = acc.shape[1]
    u_mine[...] = acc[:tokens]
    packed[:, :wide] = acc[tokens:]
    dot_m = jnp.sum(acc[:tokens] * vgs[:tokens], axis=1, keepdims=True)
    dot_t = jnp.sum(acc[tokens:] * vgs[tokens:], axis=1, keepdims=True)
    packed[:, wide : wide + HD] = jnp.broadcast_to(dot_m, (tokens, HD))
    packed[:, wide + HD : wide + 2 * HD] = jnp.broadcast_to(dot_t, (tokens, HD))
    packed[:, wide + 2 * HD :] = inverse[...]


def values_sum(mine, theirs, parts, weights, before=(), final=()):
    tokens, wide = mine.shape[1], weights[0].shape[1]
    if final:
        out = [sds((tokens, wide), F32), sds((tokens, wide + 3 * HD), F32)]
    else:
        out = sds((2 * tokens, wide), F32)
    return pl.pallas_call(
        functools.partial(values_kernel, parts=parts, first=not before, last=bool(final)),
        out_shape=out,
        compiler_params=params(),
        cost_estimate=SMALL,
        name="values",
    )(mine, theirs, *weights, *before, *final)


def first_kernel(*refs, count):
    vgs, vgs_t, gain = refs[:3]
    weights, (out_m, out_t) = refs[3 : 3 + count], refs[3 + count :]
    tokens = vgs.shape[0]
    left = both_vgs(vgs, vgs_t)
    for i in range(count):
        part = mm(left, weights[i][...], (1, 1)) * gain[i]
        out_m[i] = part[:tokens].astype(BF16)
        out_t[i] = part[tokens:].astype(BF16)


def first_terms(vgs, vgs_t, gain, weights):
    count = len(weights)
    out = sds((count, vgs.shape[0], weights[0].shape[0]), BF16)
    return pl.pallas_call(
        functools.partial(first_kernel, count=count),
        out_shape=[out, out],
        compiler_params=params(),
        cost_estimate=SMALL,
        name="first_terms",
    )(vgs, vgs_t, gain, *weights)


def local_kernel(*refs, parts, shares, width):
    mine, theirs, vgs, vgs_t, gain, inverse, own, got = refs[:8]
    weights, outs = refs[8 : 8 + len(parts)], refs[8 + len(parts) :]
    blocks = sum(shares, [])
    rows = mine.shape[2]
    tokens, wide = vgs.shape
    one, two, three = (slice(wide + i * HD, wide + (i + 1) * HD) for i in range(3))
    inv_m, inv_t = inverse[...], got[:, three]
    c_m = inv_m * inv_m * (own[:, one] + got[:, two]) / width
    c_t = inv_t * inv_t * (own[:, two] + got[:, one]) / width
    coarse = c_m.astype(BF16)
    fine = (c_m - coarse.astype(F32)).astype(BF16)
    lane = lax.broadcasted_iota(jnp.int32, c_m.shape, 1)
    outs[0][:, len(blocks) * rows :] = jnp.where(lane < HD // 2, coarse.astype(F32), fine.astype(F32)).astype(BF16)
    c_m = jnp.concatenate([c_m] * (rows // HD), axis=1)
    c_t = jnp.concatenate([c_t] * (rows // HD), axis=1)
    left = both_vgs(vgs, vgs_t)
    for part, w in zip(parts, weights, strict=True):
        r, at = part[0], span(part, rows)
        n = blocks.index(r)
        share, i = (0, n) if n < len(shares[0]) else (1, n - len(shares[0]))
        at_m = slice(n * rows + at.start, n * rows + at.stop)
        at_t = slice(i * rows + at.start, i * rows + at.stop)
        g = gain[r][:, at]
        over = 1.0 / g
        product = mm(left, w[...], (1, 1))
        h_m, h_t = features(mine, part).astype(F32), features(theirs, part).astype(F32)
        outs[0][:, at_m] = (product[:tokens] * g - h_m * over * c_m[:, at]).astype(BF16)
        outs[1 + share][:, at_t] = (product[tokens:] * g - h_t * over * c_t[:, at]).astype(BF16)


def local_grads(mine, theirs, vgs, vgs_t, gain, inverse, own, got, shares, parts, weights, width):
    tokens, rows = mine.shape[1:]
    wide = [len(share) * rows for share in shares]
    out = [sds((tokens, w), BF16) for w in (sum(wide) + HD, *wide)]
    return pl.pallas_call(
        functools.partial(local_kernel, parts=parts, shares=shares, width=width),
        out_shape=out,
        compiler_params=params(),
        cost_estimate=SMALL,
        name="local_grad",
    )(mine, theirs, vgs, vgs_t, gain, inverse, own, got, *weights)


def weight_kernel(*refs, part):
    mine, theirs, vgs, vgs_t = refs[:4]
    right = both_vgs(vgs, vgs_t)
    total = mm(pair(mine, theirs, part), right, (0, 0))
    for arrived in refs[4:-1]:
        total = total + arrived[...].astype(F32)
    refs[-1][...] = total.astype(BF16)


def weight_step(mine, theirs, vgs, vgs_t, part, arrived):
    return pl.pallas_call(
        functools.partial(weight_kernel, part=part),
        out_shape=sds((mine.shape[2] // 2, vgs.shape[1]), BF16),
        compiler_params=params(),
        cost_estimate=SMALL,
        name="weight_step",
    )(mine, theirs, vgs, vgs_t, *arrived)


def weight_last_kernel(mine, theirs, vgs, vgs_t, low_f, low_b, high_f, high_b, pin, out):
    right = both_vgs(vgs, vgs_t)
    half = low_f.shape[0]
    for side, (one, two) in enumerate(((low_f, low_b), (high_f, high_b))):
        total = mm(pair(mine, theirs, (0, side)), right, (0, 0))
        total = total + one[...].astype(F32) + two[...].astype(F32)
        out[side * half : (side + 1) * half, :] = total.astype(BF16)


def weight_last(mine, theirs, vgs, vgs_t, arrived, pin):
    return pl.pallas_call(
        weight_last_kernel,
        out_shape=sds((mine.shape[2], vgs.shape[1]), BF16),
        compiler_params=params(),
        cost_estimate=SMALL,
        name="weight_last",
    )(mine, theirs, vgs, vgs_t, *arrived, pin)


def copies_of(pieces, shares, where, out, sem, first, rows):
    copies = []
    for piece, blocks in zip(pieces, shares, strict=True):
        for j, r in enumerate(blocks):
            column = pl.multiple_of(where[first + r] * rows, rows)
            source, target = piece.at[:, j * rows : (j + 1) * rows], out.at[:, pl.ds(column, rows)]
            copies.append(pltpu.make_async_copy(source, target, sem.at[len(copies)]))
    return copies


def early_kernel(where, ones, twos, raw_m, raw_t, second, *refs, soon, shares, chips, rows):
    pieces, (out, done, sem, sems) = refs[:-4], refs[-4:]
    copies = copies_of(pieces, shares, where, out, sem, 1, rows)
    for copy in copies:
        copy.start()
    c = second[...].astype(F32)
    c = c + pltpu.roll(c, HD // 2, 1)
    c = jnp.concatenate([c] * (rows // HD), axis=1)
    for side, (terms, raw) in enumerate(((ones, raw_m), (twos, raw_t))):
        for i, r in enumerate(soon):
            done[side, i] = (terms[i].astype(F32) - raw[i].astype(F32) * c).astype(BF16)
            column = pl.multiple_of(where[1 + side * chips + r] * rows, rows)
            copies.append(pltpu.make_async_copy(done.at[side, i], out.at[:, pl.ds(column, rows)], sems.at[side, i]))
            copies[-1].start()
    for copy in copies:
        copy.wait()


def early_blocks(where, ones, twos, raw_m, raw_t, pieces, soon, shares, chips, width):
    _, tokens, rows = ones.shape
    somewhere = pl.BlockSpec(memory_space=pl.ANY)
    return pl.pallas_call(
        functools.partial(early_kernel, soon=soon, shares=shares, chips=chips, rows=rows),
        grid=(1,),
        in_specs=[
            pl.BlockSpec(memory_space=pltpu.SMEM),
            pl.BlockSpec(ones.shape, lambda i: (0, 0, 0)),
            pl.BlockSpec(twos.shape, lambda i: (0, 0, 0)),
            pl.BlockSpec(ones.shape, lambda i: (0, 0, 0)),
            pl.BlockSpec(ones.shape, lambda i: (0, 0, 0)),
            pl.BlockSpec((tokens, HD), lambda i: (0, len(shares[0]) * rows // HD)),
        ]
        + [somewhere] * len(pieces),
        out_specs=somewhere,
        out_shape=sds((tokens, width), BF16),
        scratch_shapes=[
            pltpu.VMEM((2, *ones.shape), BF16),
            pltpu.SemaphoreType.DMA((sum(len(x) for x in shares),)),
            pltpu.SemaphoreType.DMA((2, len(soon))),
        ],
        compiler_params=params(),
        cost_estimate=SMALL,
        name="early_blocks",
    )(where, ones, twos, raw_m, raw_t, pieces[0], *pieces)


def join_kernel(where, base, *refs, shares, chips, rows):
    pieces, (out, sem) = refs[:-2], refs[-2:]
    copies = copies_of(pieces, shares, where, out, sem, 1 + chips, rows)
    for copy in copies:
        copy.start()
    for copy in copies:
        copy.wait()


def join(where, base, pieces, shares, chips, rows):
    somewhere = pl.BlockSpec(memory_space=pl.ANY)
    return pl.pallas_call(
        functools.partial(join_kernel, shares=shares, chips=chips, rows=rows),
        in_specs=[pl.BlockSpec(memory_space=pltpu.SMEM)] + [somewhere] * (1 + len(pieces)),
        out_specs=somewhere,
        out_shape=sds(base.shape, BF16),
        input_output_aliases={1: 0},
        scratch_shapes=[pltpu.SemaphoreType.DMA((sum(len(x) for x in shares),))],
        compiler_params=params(),
        cost_estimate=SMALL,
        name="join",
    )(where, base, *pieces)


def fence_kernel(x, out):
    out[...] = x[...]


def fence(x, us):
    return pl.pallas_call(
        fence_kernel,
        out_shape=sds(x.shape, x.dtype),
        compiler_params=params(),
        cost_estimate=cost(us),
        name="fence",
    )(x)


def last_layer(layer_counts, layers):
    sections, mine = lax.axis_size("section"), lax.axis_index("section")
    own = layer_counts[0]
    total = own
    if sections > 2:
        reach = 1
        while reach < sections:
            route = [(i, i + reach) for i in range(sections - reach)]
            total = total + lax.ppermute(total, "section", route)
            reach *= 2
    return jnp.where(mine == sections - 1, layers, total) - 1


def shards(hidden, gain_table, layer_counts, positions, queries, keys, value_weight, out_grad):
    tokens_in, weight = hidden[0], value_weight[0]
    tokens, width = tokens_in.shape
    rows = weight.shape[0]
    sections = lax.axis_size("section")
    devices = lax.axis_size("dp")
    chips = devices // 2
    ring = list(range(0, chips, 2)) + list(range(1, chips, 2))[::-1]
    place_of = [ring.index(c) for c in range(chips)]
    me = lax.axis_index("dp")
    chip, core = me // 2, me % 2
    place = jnp.where(chip % 2 == 0, chip // 2, chips - 1 - chip // 2)
    spots = (place + jnp.arange(chips, dtype=jnp.int32)) % chips
    order = 2 * jnp.where(spots < (chips + 1) // 2, 2 * spots, 2 * (chips - 1 - spots) + 1)

    def hop(d, by):
        return 2 * ring[(place_of[d // 2] + by) % chips] + d % 2

    forth = [(d, hop(d, 1)) for d in range(devices)]
    back = [(d, hop(d, -1)) for d in range(devices)]
    swap = [(d, d ^ 1) for d in range(devices)]
    down = [(s * devices + d, (s - 1) * devices + d) for s in range(1, sections) for d in range(devices)]
    cross = [(s * devices + d, (s - 1) * devices + (d ^ 1)) for s in range(1, sections) for d in range(devices)]

    half = chips // 2
    low, high = slice(0, rows // 2), slice(rows // 2, rows)
    soon = [0, 1, chips - 1]
    later = [[2, chips - 2, 3], list(range(4, chips - 2))]

    def ahead(x):
        return lax.ppermute(x, "dp", forth)

    def behind(x):
        return lax.ppermute(x, "dp", back)

    def swapped(x):
        return lax.ppermute(x, "dp", swap)

    def sent_down(x):
        return lax.ppermute(x, ("section", "dp"), down)

    def sent_across(x):
        return lax.ppermute(x, ("section", "dp"), cross)

    token = []

    def after(x):
        x = lax.optimization_barrier((x, *token))[0] if token else x
        token[:] = [x]
        return x

    def then(*results):
        token[:] = [results[0]]
        return results if len(results) > 1 else results[0]

    pin = [jnp.zeros((8, HD), F32)]

    def hold(us=STAGE):
        pin[0] = then(fence(after(pin[0]), us))

    def parts_of(some):
        return [part for part in held if part[0] in some]

    def weights(parts):
        return [held[part] for part in parts]

    held = {(0, None): weight}
    moving = {}

    def gather_step(step):
        if step > 1:
            for r in (chips - step + 1, step - 1):
                held[r, None] = after(moving.pop(r))
        f, b = held[(chips - step + 1) % chips, None], held[step - 1, None]
        if step < half:
            moving[chips - step], moving[step] = ahead(f), behind(b)
        else:
            moving[0], moving[1] = ahead(f[low]), behind(b[high])

    gather_step(1)

    last = last_layer(layer_counts, gain_table.shape[0])
    where = jnp.concatenate([last[None], order + core, order + 1 - core]).astype(jnp.int32)
    cosine, sine = rope_tables(positions[0])
    raw_m, raw_t = then(*pick(where, tokens_in, soon, chips, rows))
    raw_m = sent_down(raw_m)
    mine, send, gain, inverse = then(*prep(after(where), tokens_in, gain_table, chips, rows))
    theirs = swapped(send)
    probs, q_rot, k_rot, vgs = then(
        *attention_probs(queries[0], keys[0], out_grad[0], cosine, sine, after(inverse))
    )
    vgs_t = swapped(vgs)
    hold(SWAP)
    gather_step(2)
    theirs, vgs_t = after(theirs), after(vgs_t)
    soon_gain = jnp.concatenate([gain[r : r + 1] for r in soon], axis=0)
    parts = parts_of(soon)
    one, two = then(*first_terms(after(vgs), vgs_t, soon_gain, [held[r, None] for r in soon]))
    raw_m = after(raw_m)
    one = sent_down(after(one))
    total = then(values_sum(after(mine), theirs, parts, weights(parts)))
    hold(RING)
    for step in range(3, half + 1):
        gather_step(step)
        if step == 3:
            one = after(one)
            two = sent_across(after(two))
        if step < half:
            parts = parts_of([step - 1, chips - step + 1])
            total = then(values_sum(after(mine), theirs, parts, weights(parts), (total,)))
            hold(RING)

    chains = [
        (0, ahead, list(range(half, 0, -1))),
        (1, behind, list(range(half, chips))),
        (1, ahead, list(range(half - 1, 0, -1))),
        (0, behind, list(range(half + 1, chips))),
    ]
    arrived = [()] * 4
    at = [0] * 4

    def weight_turn(*which):
        for i in which:
            side, move, route = chains[i]
            got = tuple(after(x) for x in arrived[i])
            part = (route[at[i]], side)
            total = then(weight_step(after(mine), theirs, vgs, vgs_t, part, got))
            arrived[i] = (move(total),)
            at[i] += 1

    hold(RING)
    two = after(two)
    raw_t = sent_down(after(raw_t))
    weight_turn(0, 1)
    parts = parts_of([half - 1, half + 1])
    total = then(values_sum(after(mine), theirs, parts, weights(parts), (total,)))
    hold(LITTLE)
    held[half, 0], held[half, 1] = after(moving[0]), after(moving[1])
    parts = parts_of([half])
    u_mine, packed = values_sum(after(mine), theirs, parts, weights(parts), (total,), (vgs, vgs_t, inverse))
    then(packed)
    got = swapped(packed)
    weight_turn(2)
    hold(PACKED)
    got = after(got)
    weight_turn(3)
    parts = parts_of(sum(later, []))
    m, t1, t2 = then(
        *local_grads(
            mine, theirs, after(vgs), vgs_t, gain, inverse, packed, got, later, parts, weights(parts), width
        )
    )
    raw_t = after(raw_t)
    m = sent_down(after(m))
    hold()
    weight_turn(0, 1)
    hold()
    weight_turn(2, 3)
    query_grad, key_grad = then(
        *attention_back(probs, q_rot, k_rot, out_grad[0], after(u_mine), got, cosine, sine, inverse)
    )
    for turn in range(2, half - 1):
        hold()
        weight_turn(0, 1)
        hold()
        weight_turn(2, 3)
        if turn == 2:
            m = after(m)
            t1 = sent_across(after(t1))
    hold()
    weight_turn(0, 1)
    last_low, last_high = after(arrived[3][0]), after(arrived[2][0])
    t2 = sent_across(after(t2))
    hold()
    upstream = then(early_blocks(where, one, two, raw_m, raw_t, [after(m)], soon, [sum(later, [])], chips, width))
    arrived = [after(arrived[0][0]), last_low, after(arrived[1][0]), last_high]
    weight_grad = then(weight_last(mine, theirs, after(vgs), vgs_t, arrived, pin[0]))
    t1, t2 = after(t1), after(t2)
    upstream = then(join(where, after(upstream), [t1, t2], later, chips, rows))
    return (query_grad[None], key_grad[None], weight_grad[None], upstream[None])


def solution(mesh):
    split = P("section", "dp", None)
    in_specs = (split, P(), P("section"), P("section", "dp"), split, split, split, split)
    out_specs = (split,) * 4
    return jax.shard_map(shards, mesh=mesh, in_specs=in_specs, out_specs=out_specs, check_vma=False)
```

```python
import functools
import math

import jax
import jax.numpy as jnp
from jax import lax
from jax.experimental import pallas as pl
from jax.experimental.pallas import tpu as pltpu
from jax.sharding import PartitionSpec as P

HQ = 32
HK = 4
HD = 128
SHARE = HQ // HK
EPS = 1e-05
F32 = jnp.float32
BF16 = jnp.bfloat16
VMEM_LIMIT = 20 * 1024 * 1024


def cost(us):
    return pl.CostEstimate(flops=int(us * 1e9) + 1, bytes_accessed=1024, transcendentals=0)


SMALL = cost(0.2)
H = [12.0, 9.0, 1.5, 1.5, 1.5, 6.0, 3.0, 6.0]


def params(**more):
    return pltpu.CompilerParams(vmem_limit_bytes=VMEM_LIMIT, **more)


def mm(a, b, contract):
    return lax.dot_general(a, b, ((contract[:1], contract[1:]), ((), ())), preferred_element_type=F32)


def sds(shape, dtype):
    return jax.ShapeDtypeStruct(shape, dtype)


def rope_tables(places):
    half = HD // 2
    steps = jnp.arange(half, dtype=F32)
    freq = jnp.exp(steps * (-2.0 * math.log(500000.0) / HD))
    angle = places.astype(F32)[:, None] * freq[None, :]
    cosine, sine = jnp.cos(angle), jnp.sin(angle)
    return jnp.concatenate([cosine, cosine], 1), jnp.concatenate([-sine, sine], 1)


def turn(x, cosine, sine):
    return x * cosine + pltpu.roll(x, HD // 2, 1) * sine


def turn_back(x, cosine, sine):
    return x * cosine - pltpu.roll(x, HD // 2, 1) * sine


def prep_kernel(
    where, mine_in, theirs_in, gain_m, gain_t, mine, theirs, gain_out, inverse, total, *, width
):
    step = pl.program_id(0)
    rows = lax.broadcasted_iota(jnp.int32, gain_m.shape, 0) == where[0]
    g_m = jnp.sum(jnp.where(rows, gain_m[...].astype(F32), 0.0), axis=0, keepdims=True)
    g_t = jnp.sum(jnp.where(rows, gain_t[...].astype(F32), 0.0), axis=0, keepdims=True)
    h_m = mine_in[...].astype(F32)
    h_t = theirs_in[...].astype(F32)
    mine[0] = (h_m * g_m).astype(BF16)
    theirs[0] = (h_t * g_t).astype(BF16)
    gain_out[0] = g_m
    part = jnp.sum(h_m * h_m + h_t * h_t, axis=1, keepdims=True)
    @pl.when(step == 0)
    def _():
        total[...] = jnp.broadcast_to(part, total.shape)

    @pl.when(step > 0)
    def _():
        total[...] += jnp.broadcast_to(part, total.shape)

    @pl.when(step == pl.num_programs(0) - 1)
    def _():
        inverse[...] = lax.rsqrt(total[...] / width + EPS)


def prep(where, hidden, gain_table, chips, rows):
    tokens, width = hidden.shape
    layers = gain_table.shape[0]
    mine = lambda r, where: (0, where[1 + r])
    theirs = lambda r, where: (0, where[1 + chips + r])
    return pl.pallas_call(
        functools.partial(prep_kernel, width=width),
        grid_spec=pltpu.PrefetchScalarGridSpec(
            num_scalar_prefetch=1,
            grid=(chips,),
            in_specs=[
                pl.BlockSpec((tokens, rows), mine),
                pl.BlockSpec((tokens, rows), theirs),
                pl.BlockSpec((layers, rows), mine),
                pl.BlockSpec((layers, rows), theirs),
            ],
            out_specs=[
                pl.BlockSpec((1, tokens, rows), lambda r, where: (r, 0, 0)),
                pl.BlockSpec((1, tokens, rows), lambda r, where: (r, 0, 0)),
                pl.BlockSpec((1, 1, rows), lambda r, where: (r, 0, 0)),
                pl.BlockSpec((tokens, HD), lambda r, where: (0, 0)),
            ],
            scratch_shapes=[pltpu.VMEM((tokens, HD), F32)],
        ),
        out_shape=[
            sds((chips, tokens, rows), BF16),
            sds((chips, tokens, rows), BF16),
            sds((chips, 1, rows), F32),
            sds((tokens, HD), F32),
        ],
        compiler_params=params(),
        cost_estimate=SMALL,
        name="prep",
    )(where, hidden, hidden, gain_table, gain_table)


def pick_kernel(where, hidden, out_m, out_t, sem, *, soon, chips):
    rows = out_m.shape[2]
    copies = []
    for side, out in enumerate((out_m, out_t)):
        for i, r in enumerate(soon):
            column = pl.multiple_of(where[1 + side * chips + r] * rows, rows)
            source = hidden.at[:, pl.ds(column, rows)]
            copies.append(pltpu.make_async_copy(source, out.at[i], sem.at[side, i]))
    for copy in copies:
        copy.start()
    for copy in copies:
        copy.wait()


def pick(where, hidden, soon, chips, rows):
    somewhere = pl.BlockSpec(memory_space=pl.ANY)
    return pl.pallas_call(
        functools.partial(pick_kernel, soon=soon, chips=chips),
        in_specs=[pl.BlockSpec(memory_space=pltpu.SMEM), somewhere],
        out_specs=[somewhere, somewhere],
        out_shape=[sds((len(soon), hidden.shape[0], rows), BF16)] * 2,
        scratch_shapes=[pltpu.SemaphoreType.DMA((2, len(soon)))],
        compiler_params=params(),
        cost_estimate=SMALL,
        name="pick",
    )(where, hidden)


def stacked(ref):
    return jnp.concatenate([ref[:, h * HD : (h + 1) * HD] for h in range(SHARE)], axis=0)


def probs_kernel(q_ref, k_ref, d_ref, cosine, sine, inverse, probs, q_out, k_out, vgs):
    cos, sin = cosine[...], sine[...]
    tokens = k_ref.shape[0]
    k_rot = turn(k_ref[...].astype(F32), cos, sin).astype(BF16)
    q_rot = jnp.concatenate(
        [turn(q_ref[:, h * HD : (h + 1) * HD].astype(F32), cos, sin).astype(BF16) for h in range(SHARE)],
        axis=0,
    )
    q_out[0] = q_rot
    k_out[0] = k_rot
    scores = mm(k_rot, q_rot, (1, 1)) * (HD**-0.5)
    key_at = lax.broadcasted_iota(jnp.int32, (tokens, tokens), 0)
    query_at = lax.broadcasted_iota(jnp.int32, (tokens, tokens), 1)
    seen = key_at <= query_at
    lows = []
    for h in range(SHARE):
        s = jnp.where(seen, scores[:, h * tokens : (h + 1) * tokens], -1e30)
        e = jnp.exp(s - jnp.max(s, axis=0, keepdims=True))
        p = e / jnp.sum(e, axis=0, keepdims=True)
        probs[0, :, h * tokens : (h + 1) * tokens] = p
        lows.append(p.astype(BF16))
    grad = mm(jnp.concatenate(lows, axis=1), stacked(d_ref), (1, 0))
    vgs[...] = (grad * inverse[...]).astype(BF16)


def attention_probs(queries, keys, out_grad, cosine, sine, inverse):
    tokens = queries.shape[0]
    group = pl.BlockSpec((tokens, SHARE * HD), lambda g: (0, g))
    head = pl.BlockSpec((tokens, HD), lambda g: (0, g))
    table = pl.BlockSpec((tokens, HD), lambda g: (0, 0))
    return pl.pallas_call(
        probs_kernel,
        grid=(HK,),
        in_specs=[group, head, group, table, table, table],
        out_specs=[
            pl.BlockSpec((1, tokens, SHARE * tokens), lambda g: (g, 0, 0)),
            pl.BlockSpec((1, SHARE * tokens, HD), lambda g: (g, 0, 0)),
            pl.BlockSpec((1, tokens, HD), lambda g: (g, 0, 0)),
            head,
        ],
        out_shape=[
            pltpu.HBM((HK, tokens, SHARE * tokens), F32),
            pltpu.HBM((HK, SHARE * tokens, HD), BF16),
            pltpu.HBM((HK, tokens, HD), BF16),
            sds((tokens, HK * HD), BF16),
        ],
        compiler_params=params(),
        cost_estimate=SMALL,
        name="probs",
    )(queries, keys, out_grad, cosine, sine, inverse)


def back_kernel(probs, q_rot, k_rot, d_ref, u_one, u_two, cosine, sine, inverse, dq, dk):
    cos, sin = cosine[...], sine[...]
    tokens = k_rot.shape[1]
    values = ((u_one[...] + u_two[...]) * inverse[...]).astype(BF16)
    d_probs = mm(values, stacked(d_ref), (1, 1))
    p = probs[0]
    delta = jnp.sum(p.astype(BF16).astype(F32) * d_probs, axis=0, keepdims=True)
    d_scores = (p * (d_probs - delta) * (HD**-0.5)).astype(BF16)
    dk[...] = turn_back(mm(d_scores, q_rot[0], (1, 0)), cos, sin).astype(BF16)
    key = k_rot[0]
    for h in range(SHARE):
        part = mm(d_scores[:, h * tokens : (h + 1) * tokens], key, (0, 0))
        dq[:, h * HD : (h + 1) * HD] = turn_back(part, cos, sin).astype(BF16)


def attention_back(probs, q_rot, k_rot, out_grad, u_one, u_two, cosine, sine, inverse):
    tokens = out_grad.shape[0]
    group = pl.BlockSpec((tokens, SHARE * HD), lambda g: (0, g))
    head = pl.BlockSpec((tokens, HD), lambda g: (0, g))
    table = pl.BlockSpec((tokens, HD), lambda g: (0, 0))
    return pl.pallas_call(
        back_kernel,
        grid=(HK,),
        in_specs=[
            pl.BlockSpec((1, tokens, SHARE * tokens), lambda g: (g, 0, 0)),
            pl.BlockSpec((1, SHARE * tokens, HD), lambda g: (g, 0, 0)),
            pl.BlockSpec((1, tokens, HD), lambda g: (g, 0, 0)),
            group,
            head,
            head,
            table,
            table,
            table,
        ],
        out_specs=[group, head],
        out_shape=[sds((tokens, HQ * HD), BF16), sds((tokens, HK * HD), BF16)],
        compiler_params=params(),
        cost_estimate=SMALL,
        name="back",
    )(probs, q_rot, k_rot, out_grad, u_one, u_two, cosine, sine, inverse)


def span(part, rows):
    side = part[1]
    return slice(0, rows) if side is None else slice(side * rows // 2, (side + 1) * rows // 2)


def features(ref, part):
    return ref[part[0]][:, span(part, ref.shape[2])]


def both_vgs(vgs, vgs_t):
    return jnp.concatenate([vgs[...], vgs_t[...]], axis=0)


def pair(mine, theirs, part):
    return jnp.concatenate([features(mine, part), features(theirs, part)], axis=0)


def values_kernel(*refs, parts, first, last):
    mine, theirs = refs[0], refs[1]
    weights, rest = refs[2 : 2 + len(parts)], refs[2 + len(parts) :]
    tokens = mine.shape[1]
    acc = None
    if not first:
        acc, rest = rest[0][...], rest[1:]
    for part, w in zip(parts, weights, strict=True):
        product = mm(pair(mine, theirs, part), w[...], (1, 0))
        acc = product if acc is None else acc + product
    if not last:
        rest[0][...] = acc
        return
    vgs, vgs_t, inverse, u_mine, packed = rest
    vgs = both_vgs(vgs, vgs_t).astype(F32)
    wide = acc.shape[1]
    u_mine[...] = acc[:tokens]
    packed[:, :wide] = acc[tokens:]
    dot_m = jnp.sum(acc[:tokens] * vgs[:tokens], axis=1, keepdims=True)
    dot_t = jnp.sum(acc[tokens:] * vgs[tokens:], axis=1, keepdims=True)
    packed[:, wide : wide + HD] = jnp.broadcast_to(dot_m, (tokens, HD))
    packed[:, wide + HD : wide + 2 * HD] = jnp.broadcast_to(dot_t, (tokens, HD))
    packed[:, wide + 2 * HD :] = inverse[...]


def values_sum(mine, theirs, parts, weights, before=(), final=()):
    tokens, wide = mine.shape[1], weights[0].shape[1]
    if final:
        out = [sds((tokens, wide), F32), sds((tokens, wide + 3 * HD), F32)]
    else:
        out = sds((2 * tokens, wide), F32)
    return pl.pallas_call(
        functools.partial(values_kernel, parts=parts, first=not before, last=bool(final)),
        out_shape=out,
        compiler_params=params(),
        cost_estimate=SMALL,
        name="values",
    )(mine, theirs, *weights, *before, *final)


def first_kernel(*refs, count):
    vgs, vgs_t, gain = refs[:3]
    weights, (out_m, out_t) = refs[3 : 3 + count], refs[3 + count :]
    tokens = vgs.shape[0]
    left = both_vgs(vgs, vgs_t)
    for i in range(count):
        part = mm(left, weights[i][...], (1, 1)) * gain[i]
        out_m[i] = part[:tokens].astype(BF16)
        out_t[i] = part[tokens:].astype(BF16)


def first_terms(vgs, vgs_t, gain, weights):
    count = len(weights)
    out = sds((count, vgs.shape[0], weights[0].shape[0]), BF16)
    return pl.pallas_call(
        functools.partial(first_kernel, count=count),
        out_shape=[out, out],
        compiler_params=params(),
        cost_estimate=SMALL,
        name="first_terms",
    )(vgs, vgs_t, gain, *weights)


def local_kernel(*refs, parts, shares, width):
    mine, theirs, vgs, vgs_t, gain, inverse, own, got = refs[:8]
    weights, outs = refs[8 : 8 + len(parts)], refs[8 + len(parts) :]
    blocks = sum(shares, [])
    rows = mine.shape[2]
    tokens, wide = vgs.shape
    one, two, three = (slice(wide + i * HD, wide + (i + 1) * HD) for i in range(3))
    inv_m, inv_t = inverse[...], got[:, three]
    c_m = inv_m * inv_m * (own[:, one] + got[:, two]) / width
    c_t = inv_t * inv_t * (own[:, two] + got[:, one]) / width
    coarse = c_m.astype(BF16)
    fine = (c_m - coarse.astype(F32)).astype(BF16)
    lane = lax.broadcasted_iota(jnp.int32, c_m.shape, 1)
    outs[0][:, len(blocks) * rows :] = jnp.where(lane < HD // 2, coarse.astype(F32), fine.astype(F32)).astype(BF16)
    c_m = jnp.concatenate([c_m] * (rows // HD), axis=1)
    c_t = jnp.concatenate([c_t] * (rows // HD), axis=1)
    left = both_vgs(vgs, vgs_t)
    for part, w in zip(parts, weights, strict=True):
        r, at = part[0], span(part, rows)
        n = blocks.index(r)
        to = slice(n * rows + at.start, n * rows + at.stop)
        g = gain[r][:, at]
        over = 1.0 / g
        product = mm(left, w[...], (1, 1))
        h_m, h_t = features(mine, part).astype(F32), features(theirs, part).astype(F32)
        outs[0][:, to] = (product[:tokens] * g - h_m * over * c_m[:, at]).astype(BF16)
        outs[1][:, to] = (product[tokens:] * g - h_t * over * c_t[:, at]).astype(BF16)


def local_grads(mine, theirs, vgs, vgs_t, gain, inverse, own, got, shares, parts, weights, width):
    tokens, rows = mine.shape[1:]
    wide = sum(len(share) for share in shares) * rows
    out = [sds((tokens, wide + HD), BF16), sds((tokens, wide), BF16)]
    return pl.pallas_call(
        functools.partial(local_kernel, parts=parts, shares=shares, width=width),
        out_shape=out,
        compiler_params=params(),
        cost_estimate=SMALL,
        name="local_grad",
    )(mine, theirs, vgs, vgs_t, gain, inverse, own, got, *weights)


def weight_kernel(*refs, part):
    mine, theirs, vgs, vgs_t = refs[:4]
    out = refs[-1]
    total = mm(pair(mine, theirs, part), both_vgs(vgs, vgs_t), (0, 0))
    rows = total.shape[0]
    for side, arrived in enumerate(refs[4:-1]):
        if arrived is None:
            continue
        if arrived.shape[0] == rows:
            total = total + arrived[...].astype(F32)
        elif side == 0:
            total = jnp.concatenate([total[: rows // 2] + arrived[...].astype(F32), total[rows // 2 :]], axis=0)
        else:
            total = jnp.concatenate([total[: rows // 2], total[rows // 2 :] + arrived[...].astype(F32)], axis=0)
    out[...] = total.astype(BF16)


def weight_step(mine, theirs, vgs, vgs_t, part, from_behind=None, from_ahead=None):
    at = span(part, mine.shape[2])

    def kernel(*refs):
        refs = list(refs)
        if from_behind is None:
            refs.insert(4, None)
        if from_ahead is None:
            refs.insert(5, None)
        weight_kernel(*refs, part=part)

    arrived = [x for x in (from_behind, from_ahead) if x is not None]
    return pl.pallas_call(
        kernel,
        out_shape=sds((at.stop - at.start, vgs.shape[1]), BF16),
        compiler_params=params(),
        cost_estimate=SMALL,
        name="weight_step",
    )(mine, theirs, vgs, vgs_t, *arrived)


def copies_of(pieces, shares, where, out, sem, first, rows):
    copies = []
    for piece, blocks in zip(pieces, shares, strict=True):
        for j, r in enumerate(blocks):
            column = pl.multiple_of(where[first + r] * rows, rows)
            source, target = piece.at[:, j * rows : (j + 1) * rows], out.at[:, pl.ds(column, rows)]
            copies.append(pltpu.make_async_copy(source, target, sem.at[len(copies)]))
    return copies


def early_kernel(where, pin, ones, twos, raw_m, raw_t, second, *refs, soon, shares, chips, rows):
    pieces, (out, done, sem, sems) = refs[:-4], refs[-4:]
    copies = copies_of(pieces, shares, where, out, sem, 1, rows)
    for copy in copies:
        copy.start()
    c = second[...].astype(F32)
    c = c + pltpu.roll(c, HD // 2, 1)
    c = jnp.concatenate([c] * (rows // HD), axis=1)
    for side, (terms, raw) in enumerate(((ones, raw_m), (twos, raw_t))):
        for i, r in enumerate(soon):
            done[side, i] = (terms[i].astype(F32) - raw[i].astype(F32) * c).astype(BF16)
            column = pl.multiple_of(where[1 + side * chips + r] * rows, rows)
            copies.append(pltpu.make_async_copy(done.at[side, i], out.at[:, pl.ds(column, rows)], sems.at[side, i]))
            copies[-1].start()
    for copy in copies:
        copy.wait()


def early_blocks(where, pin, ones, twos, raw_m, raw_t, pieces, soon, shares, chips, width):
    _, tokens, rows = ones.shape
    somewhere = pl.BlockSpec(memory_space=pl.ANY)
    return pl.pallas_call(
        functools.partial(early_kernel, soon=soon, shares=shares, chips=chips, rows=rows),
        grid=(1,),
        in_specs=[
            pl.BlockSpec(memory_space=pltpu.SMEM),
            somewhere,
            pl.BlockSpec(ones.shape, lambda i: (0, 0, 0)),
            pl.BlockSpec(twos.shape, lambda i: (0, 0, 0)),
            pl.BlockSpec(ones.shape, lambda i: (0, 0, 0)),
            pl.BlockSpec(ones.shape, lambda i: (0, 0, 0)),
            pl.BlockSpec((tokens, HD), lambda i: (0, len(shares[0]) * rows // HD)),
        ]
        + [somewhere] * len(pieces),
        out_specs=somewhere,
        out_shape=sds((tokens, width), BF16),
        scratch_shapes=[
            pltpu.VMEM((2, *ones.shape), BF16),
            pltpu.SemaphoreType.DMA((sum(len(x) for x in shares),)),
            pltpu.SemaphoreType.DMA((2, len(soon))),
        ],
        compiler_params=params(),
        cost_estimate=SMALL,
        name="early_blocks",
    )(where, pin, ones, twos, raw_m, raw_t, pieces[0], *pieces)


def join_kernel(where, base, *refs, shares, chips, rows):
    pieces, (out, sem) = refs[:-2], refs[-2:]
    copies = copies_of(pieces, shares, where, out, sem, 1 + chips, rows)
    for copy in copies:
        copy.start()
    for copy in copies:
        copy.wait()


def join(where, base, pieces, shares, chips, rows):
    somewhere = pl.BlockSpec(memory_space=pl.ANY)
    return pl.pallas_call(
        functools.partial(join_kernel, shares=shares, chips=chips, rows=rows),
        in_specs=[pl.BlockSpec(memory_space=pltpu.SMEM)] + [somewhere] * (1 + len(pieces)),
        out_specs=somewhere,
        out_shape=sds(base.shape, BF16),
        input_output_aliases={1: 0},
        scratch_shapes=[pltpu.SemaphoreType.DMA((sum(len(x) for x in shares),))],
        compiler_params=params(),
        cost_estimate=SMALL,
        name="join",
    )(where, base, *pieces)


def fence_kernel(x, out):
    out[...] = x[...]


def fence(x, us):
    return pl.pallas_call(
        fence_kernel,
        out_shape=sds(x.shape, x.dtype),
        compiler_params=params(),
        cost_estimate=cost(us),
        name="fence",
    )(x)


def last_layer(layer_counts, layers):
    sections, mine = lax.axis_size("section"), lax.axis_index("section")
    own = layer_counts[0]
    total = own
    if sections > 2:
        reach = 1
        while reach < sections:
            route = [(i, i + reach) for i in range(sections - reach)]
            total = total + lax.ppermute(total, "section", route)
            reach *= 2
    return jnp.where(mine == sections - 1, layers, total) - 1


def shards(hidden, gain_table, layer_counts, positions, queries, keys, value_weight, out_grad):
    tokens_in, weight = hidden[0], value_weight[0]
    tokens, width = tokens_in.shape
    rows = weight.shape[0]
    sections = lax.axis_size("section")
    devices = lax.axis_size("dp")
    chips = devices // 2
    ring = list(range(0, chips, 2)) + list(range(1, chips, 2))[::-1]
    place_of = [ring.index(c) for c in range(chips)]
    me = lax.axis_index("dp")
    chip, core = me // 2, me % 2
    place = jnp.where(chip % 2 == 0, chip // 2, chips - 1 - chip // 2)
    spots = (place + jnp.arange(chips, dtype=jnp.int32)) % chips
    order = 2 * jnp.where(spots < (chips + 1) // 2, 2 * spots, 2 * (chips - 1 - spots) + 1)

    def hop(d, by):
        return 2 * ring[(place_of[d // 2] + by) % chips] + d % 2

    forth = [(d, hop(d, 1)) for d in range(devices)]
    back = [(d, hop(d, -1)) for d in range(devices)]
    swap = [(d, d ^ 1) for d in range(devices)]
    down = [(s * devices + d, (s - 1) * devices + d) for s in range(1, sections) for d in range(devices)]
    cross = [(s * devices + d, (s - 1) * devices + (d ^ 1)) for s in range(1, sections) for d in range(devices)]

    half = chips // 2
    low, high = slice(0, rows // 2), slice(rows // 2, rows)
    soon = [0, 1, chips - 1]
    later = [[2, chips - 2, 3], list(range(4, chips - 2))]

    def ahead(x):
        return lax.ppermute(x, "dp", forth)

    def behind(x):
        return lax.ppermute(x, "dp", back)

    def swapped(x):
        return lax.ppermute(x, "dp", swap)

    def sent_down(x):
        return lax.ppermute(x, ("section", "dp"), down)

    def sent_across(x):
        return lax.ppermute(x, ("section", "dp"), cross)

    token = []

    def after(x):
        x = lax.optimization_barrier((x, *token))[0] if token else x
        token[:] = [x]
        return x

    def then(*results):
        token[:] = [results[0]]
        return results if len(results) > 1 else results[0]

    pin = [jnp.zeros((8, HD), F32)]

    def hold(us):
        pin[0] = then(fence(after(pin[0]), us))

    def parts_of(some):
        return [part for part in held if part[0] in some]

    def weights(parts):
        return [held[part] for part in parts]

    held = {(0, None): weight}
    moving = {(chips - 1, None): ahead(weight), (1, None): behind(weight)}

    def gather_next(step, side):
        for r, back_r, half_side, move in ((chips - step, chips - step + 1, side, ahead), (step, step - 1, 1 - side, behind)):
            if step == 2:
                source = held[back_r, None][high if half_side else low]
            else:
                source = held[back_r, half_side]
            moving[r, half_side] = move(source)

    def gather_here(step, side):
        for key in ((chips - step, side), (step, 1 - side)):
            held[key] = after(moving.pop(key))

    last = last_layer(layer_counts, gain_table.shape[0])
    where = jnp.concatenate([last[None], order + core, order + 1 - core]).astype(jnp.int32)
    cosine, sine = rope_tables(positions[0])
    raw_m, raw_t = then(*pick(where, tokens_in, soon, chips, rows))
    raw_m = sent_down(raw_m)
    mine, send, gain, inverse = then(*prep(after(where), tokens_in, gain_table, chips, rows))
    theirs = swapped(send)
    probs, q_rot, k_rot, vgs = then(
        *attention_probs(queries[0], keys[0], out_grad[0], cosine, sine, after(inverse))
    )
    vgs_t = swapped(vgs)
    hold(H[0])
    for key in ((chips - 1, None), (1, None)):
        held[key] = after(moving.pop(key))
    gather_next(2, 0)
    theirs, vgs_t = after(theirs), after(vgs_t)
    soon_gain = jnp.concatenate([gain[r : r + 1] for r in soon], axis=0)
    parts = parts_of(soon)
    one, two = then(*first_terms(after(vgs), vgs_t, soon_gain, [held[r, None] for r in soon]))
    late = {r: after(held[r, None]) for r in (chips - 1, 1)}
    moving[chips - 2, 1] = ahead(late[chips - 1][high])
    moving[2, 0] = behind(late[1][low])
    raw_m = after(raw_m)
    one = sent_down(after(one))
    total = then(values_sum(after(mine), theirs, parts, weights(parts)))
    hold(H[1])
    for step in range(2, half):
        gather_here(step, 0)
        if step + 1 <= half:
            gather_next(step + 1, 0)
        hold(H[2])
        gather_here(step, 1)
        if step + 1 < half:
            gather_next(step + 1, 1)
        if step == 2:
            one = after(one)
            two = sent_across(after(two))
        if step < half - 1:
            parts = parts_of([step, chips - step])
            total = then(values_sum(after(mine), theirs, parts, weights(parts), (total,)))
            hold(H[3])

    def weight_part(part, *arrived):
        return then(weight_step(after(mine), theirs, vgs, vgs_t, part, *arrived))

    f = ahead(weight_part((half, 0)))
    b = behind(weight_part((half, 1)))
    two = after(two)
    raw_t = sent_down(after(raw_t))
    hold(H[4])
    parts = parts_of([half - 1, half + 1])
    total = then(values_sum(after(mine), theirs, parts, weights(parts), (total,)))
    for key in ((half, 0), (half, 1)):
        held[key] = after(moving.pop(key))
    parts = parts_of([half])
    u_mine, packed = values_sum(after(mine), theirs, parts, weights(parts), (total,), (vgs, vgs_t, inverse))
    got = swapped(then(packed))

    def weight_turn(r, f, b):
        f, b = after(f), after(b)
        return ahead(weight_part((r, None), f)), behind(weight_part((chips - r, None), None, b))

    if half > 2:
        f, b = weight_turn(half - 1, f, b)
    hold(H[5])
    got = after(got)
    parts = parts_of(sum(later, []))
    m, t = then(
        *local_grads(
            mine, theirs, after(vgs), vgs_t, gain, inverse, packed, got, later, parts, weights(parts), width
        )
    )
    m, t = sent_down(m), sent_across(t)
    query_grad, key_grad = then(
        *attention_back(probs, q_rot, k_rot, out_grad[0], after(u_mine), got, cosine, sine, inverse)
    )
    hold(H[6])
    for r in range(half - 2, 0, -1):
        f, b = weight_turn(r, f, b)
        if r == 2:
            raw_t = after(raw_t)
        hold(H[7])
    upstream = then(
        early_blocks(where, pin[0], one, two, raw_m, raw_t, [after(m)], soon, [sum(later, [])], chips, width)
    )
    t = after(t)
    upstream = then(join(where, after(upstream), [t], [sum(later, [])], chips, rows))
    f, b = after(f), after(b)
    weight_grad = weight_step(mine, theirs, vgs, vgs_t, (0, None), f, b)
    return (query_grad[None], key_grad[None], weight_grad[None], upstream[None])


def solution(mesh):
    split = P("section", "dp", None)
    in_specs = (split, P(), P("section"), P("section", "dp"), split, split, split, split)
    out_specs = (split,) * 4
    return jax.shard_map(shards, mesh=mesh, in_specs=in_specs, out_specs=out_specs, check_vma=False)
```

```python
import functools
import math

import jax
import jax.numpy as jnp
from jax import lax
from jax.experimental import pallas as pl
from jax.experimental.pallas import tpu as pltpu
from jax.sharding import PartitionSpec as P

HQ = 32
HK = 4
HD = 128
SHARE = HQ // HK
EPS = 1e-05
F32 = jnp.float32
BF16 = jnp.bfloat16
VMEM_LIMIT = 20 * 1024 * 1024


def cost(us):
    return pl.CostEstimate(flops=int(us * 1e9) + 1, bytes_accessed=1024, transcendentals=0)


SMALL = cost(0.2)
H = [12.0, 9.0, 1.5, 1.5, 1.5, 6.0, 3.0, 6.0]


def params(**more):
    return pltpu.CompilerParams(vmem_limit_bytes=VMEM_LIMIT, **more)


def mm(a, b, contract):
    return lax.dot_general(a, b, ((contract[:1], contract[1:]), ((), ())), preferred_element_type=F32)


def sds(shape, dtype):
    return jax.ShapeDtypeStruct(shape, dtype)


def rope_tables(places):
    half = HD // 2
    steps = jnp.arange(half, dtype=F32)
    freq = jnp.exp(steps * (-2.0 * math.log(500000.0) / HD))
    angle = places.astype(F32)[:, None] * freq[None, :]
    cosine, sine = jnp.cos(angle), jnp.sin(angle)
    return jnp.concatenate([cosine, cosine], 1), jnp.concatenate([-sine, sine], 1)


def turn(x, cosine, sine):
    return x * cosine + pltpu.roll(x, HD // 2, 1) * sine


def turn_back(x, cosine, sine):
    return x * cosine - pltpu.roll(x, HD // 2, 1) * sine


def prep_kernel(
    where, mine_in, theirs_in, gain_m, gain_t, mine, theirs, gain_out, inverse, total, *, width
):
    step = pl.program_id(0)
    rows = lax.broadcasted_iota(jnp.int32, gain_m.shape, 0) == where[0]
    g_m = jnp.sum(jnp.where(rows, gain_m[...].astype(F32), 0.0), axis=0, keepdims=True)
    g_t = jnp.sum(jnp.where(rows, gain_t[...].astype(F32), 0.0), axis=0, keepdims=True)
    h_m = mine_in[...].astype(F32)
    h_t = theirs_in[...].astype(F32)
    mine[0] = (h_m * g_m).astype(BF16)
    theirs[0] = (h_t * g_t).astype(BF16)
    gain_out[0] = g_m
    part = jnp.sum(h_m * h_m + h_t * h_t, axis=1, keepdims=True)
    @pl.when(step == 0)
    def _():
        total[...] = jnp.broadcast_to(part, total.shape)

    @pl.when(step > 0)
    def _():
        total[...] += jnp.broadcast_to(part, total.shape)

    @pl.when(step == pl.num_programs(0) - 1)
    def _():
        inverse[...] = lax.rsqrt(total[...] / width + EPS)


def prep(where, hidden, gain_table, chips, rows):
    tokens, width = hidden.shape
    layers = gain_table.shape[0]
    mine = lambda r, where: (0, where[1 + r])
    theirs = lambda r, where: (0, where[1 + chips + r])
    return pl.pallas_call(
        functools.partial(prep_kernel, width=width),
        grid_spec=pltpu.PrefetchScalarGridSpec(
            num_scalar_prefetch=1,
            grid=(chips,),
            in_specs=[
                pl.BlockSpec((tokens, rows), mine),
                pl.BlockSpec((tokens, rows), theirs),
                pl.BlockSpec((layers, rows), mine),
                pl.BlockSpec((layers, rows), theirs),
            ],
            out_specs=[
                pl.BlockSpec((1, tokens, rows), lambda r, where: (r, 0, 0)),
                pl.BlockSpec((1, tokens, rows), lambda r, where: (r, 0, 0)),
                pl.BlockSpec((1, 1, rows), lambda r, where: (r, 0, 0)),
                pl.BlockSpec((tokens, HD), lambda r, where: (0, 0)),
            ],
            scratch_shapes=[pltpu.VMEM((tokens, HD), F32)],
        ),
        out_shape=[
            sds((chips, tokens, rows), BF16),
            sds((chips, tokens, rows), BF16),
            sds((chips, 1, rows), F32),
            sds((tokens, HD), F32),
        ],
        compiler_params=params(),
        cost_estimate=SMALL,
        name="prep",
    )(where, hidden, hidden, gain_table, gain_table)


def pick_kernel(where, hidden, out_m, out_t, sem, *, soon, chips):
    rows = out_m.shape[2]
    copies = []
    for side, out in enumerate((out_m, out_t)):
        for i, r in enumerate(soon):
            column = pl.multiple_of(where[1 + side * chips + r] * rows, rows)
            source = hidden.at[:, pl.ds(column, rows)]
            copies.append(pltpu.make_async_copy(source, out.at[i], sem.at[side, i]))
    for copy in copies:
        copy.start()
    for copy in copies:
        copy.wait()


def pick(where, hidden, soon, chips, rows):
    somewhere = pl.BlockSpec(memory_space=pl.ANY)
    return pl.pallas_call(
        functools.partial(pick_kernel, soon=soon, chips=chips),
        in_specs=[pl.BlockSpec(memory_space=pltpu.SMEM), somewhere],
        out_specs=[somewhere, somewhere],
        out_shape=[sds((len(soon), hidden.shape[0], rows), BF16)] * 2,
        scratch_shapes=[pltpu.SemaphoreType.DMA((2, len(soon)))],
        compiler_params=params(),
        cost_estimate=SMALL,
        name="pick",
    )(where, hidden)


def stacked(ref):
    return jnp.concatenate([ref[:, h * HD : (h + 1) * HD] for h in range(SHARE)], axis=0)


def probs_kernel(q_ref, k_ref, d_ref, cosine, sine, inverse, probs, q_out, k_out, vgs):
    cos, sin = cosine[...], sine[...]
    tokens = k_ref.shape[0]
    k_rot = turn(k_ref[...].astype(F32), cos, sin).astype(BF16)
    q_rot = jnp.concatenate(
        [turn(q_ref[:, h * HD : (h + 1) * HD].astype(F32), cos, sin).astype(BF16) for h in range(SHARE)],
        axis=0,
    )
    q_out[0] = q_rot
    k_out[0] = k_rot
    scores = mm(k_rot, q_rot, (1, 1)) * (HD**-0.5)
    key_at = lax.broadcasted_iota(jnp.int32, (tokens, tokens), 0)
    query_at = lax.broadcasted_iota(jnp.int32, (tokens, tokens), 1)
    seen = key_at <= query_at
    lows = []
    for h in range(SHARE):
        s = jnp.where(seen, scores[:, h * tokens : (h + 1) * tokens], -1e30)
        e = jnp.exp(s - jnp.max(s, axis=0, keepdims=True))
        p = e / jnp.sum(e, axis=0, keepdims=True)
        probs[0, :, h * tokens : (h + 1) * tokens] = p
        lows.append(p.astype(BF16))
    grad = mm(jnp.concatenate(lows, axis=1), stacked(d_ref), (1, 0))
    vgs[...] = (grad * inverse[...]).astype(BF16)


def attention_probs(queries, keys, out_grad, cosine, sine, inverse):
    tokens = queries.shape[0]
    group = pl.BlockSpec((tokens, SHARE * HD), lambda g: (0, g))
    head = pl.BlockSpec((tokens, HD), lambda g: (0, g))
    table = pl.BlockSpec((tokens, HD), lambda g: (0, 0))
    return pl.pallas_call(
        probs_kernel,
        grid=(HK,),
        in_specs=[group, head, group, table, table, table],
        out_specs=[
            pl.BlockSpec((1, tokens, SHARE * tokens), lambda g: (g, 0, 0)),
            pl.BlockSpec((1, SHARE * tokens, HD), lambda g: (g, 0, 0)),
            pl.BlockSpec((1, tokens, HD), lambda g: (g, 0, 0)),
            head,
        ],
        out_shape=[
            pltpu.HBM((HK, tokens, SHARE * tokens), F32),
            pltpu.HBM((HK, SHARE * tokens, HD), BF16),
            pltpu.HBM((HK, tokens, HD), BF16),
            sds((tokens, HK * HD), BF16),
        ],
        compiler_params=params(),
        cost_estimate=SMALL,
        name="probs",
    )(queries, keys, out_grad, cosine, sine, inverse)


def back_kernel(probs, q_rot, k_rot, d_ref, u_one, u_two, cosine, sine, inverse, dq, dk):
    cos, sin = cosine[...], sine[...]
    tokens = k_rot.shape[1]
    values = ((u_one[...] + u_two[...]) * inverse[...]).astype(BF16)
    d_probs = mm(values, stacked(d_ref), (1, 1))
    p = probs[0]
    delta = jnp.sum(p.astype(BF16).astype(F32) * d_probs, axis=0, keepdims=True)
    d_scores = (p * (d_probs - delta) * (HD**-0.5)).astype(BF16)
    dk[...] = turn_back(mm(d_scores, q_rot[0], (1, 0)), cos, sin).astype(BF16)
    key = k_rot[0]
    for h in range(SHARE):
        part = mm(d_scores[:, h * tokens : (h + 1) * tokens], key, (0, 0))
        dq[:, h * HD : (h + 1) * HD] = turn_back(part, cos, sin).astype(BF16)


def attention_back(probs, q_rot, k_rot, out_grad, u_one, u_two, cosine, sine, inverse):
    tokens = out_grad.shape[0]
    group = pl.BlockSpec((tokens, SHARE * HD), lambda g: (0, g))
    head = pl.BlockSpec((tokens, HD), lambda g: (0, g))
    table = pl.BlockSpec((tokens, HD), lambda g: (0, 0))
    return pl.pallas_call(
        back_kernel,
        grid=(HK,),
        in_specs=[
            pl.BlockSpec((1, tokens, SHARE * tokens), lambda g: (g, 0, 0)),
            pl.BlockSpec((1, SHARE * tokens, HD), lambda g: (g, 0, 0)),
            pl.BlockSpec((1, tokens, HD), lambda g: (g, 0, 0)),
            group,
            head,
            head,
            table,
            table,
            table,
        ],
        out_specs=[group, head],
        out_shape=[sds((tokens, HQ * HD), BF16), sds((tokens, HK * HD), BF16)],
        compiler_params=params(),
        cost_estimate=SMALL,
        name="back",
    )(probs, q_rot, k_rot, out_grad, u_one, u_two, cosine, sine, inverse)


def span(part, rows):
    side = part[1]
    return slice(0, rows) if side is None else slice(side * rows // 2, (side + 1) * rows // 2)


def features(ref, part):
    return ref[part[0]][:, span(part, ref.shape[2])]


def both_vgs(vgs, vgs_t):
    return jnp.concatenate([vgs[...], vgs_t[...]], axis=0)


def pair(mine, theirs, part):
    return jnp.concatenate([features(mine, part), features(theirs, part)], axis=0)


def values_kernel(*refs, parts, first, last):
    mine, theirs = refs[0], refs[1]
    weights, rest = refs[2 : 2 + len(parts)], refs[2 + len(parts) :]
    tokens = mine.shape[1]
    acc = None
    if not first:
        acc, rest = rest[0][...], rest[1:]
    for part, w in zip(parts, weights, strict=True):
        product = mm(pair(mine, theirs, part), w[...], (1, 0))
        acc = product if acc is None else acc + product
    if not last:
        rest[0][...] = acc
        return
    vgs, vgs_t, inverse, u_mine, packed = rest
    vgs = both_vgs(vgs, vgs_t).astype(F32)
    wide = acc.shape[1]
    u_mine[...] = acc[:tokens]
    packed[:, :wide] = acc[tokens:]
    dot_m = jnp.sum(acc[:tokens] * vgs[:tokens], axis=1, keepdims=True)
    dot_t = jnp.sum(acc[tokens:] * vgs[tokens:], axis=1, keepdims=True)
    packed[:, wide : wide + HD] = jnp.broadcast_to(dot_m, (tokens, HD))
    packed[:, wide + HD : wide + 2 * HD] = jnp.broadcast_to(dot_t, (tokens, HD))
    packed[:, wide + 2 * HD :] = inverse[...]


def values_sum(mine, theirs, parts, weights, before=(), final=()):
    tokens, wide = mine.shape[1], weights[0].shape[1]
    if final:
        out = [sds((tokens, wide), F32), sds((tokens, wide + 3 * HD), F32)]
    else:
        out = sds((2 * tokens, wide), F32)
    return pl.pallas_call(
        functools.partial(values_kernel, parts=parts, first=not before, last=bool(final)),
        out_shape=out,
        compiler_params=params(),
        cost_estimate=SMALL,
        name="values",
    )(mine, theirs, *weights, *before, *final)


def first_kernel(*refs, count):
    vgs, vgs_t, gain = refs[:3]
    weights, (out_m, out_t) = refs[3 : 3 + count], refs[3 + count :]
    tokens = vgs.shape[0]
    left = both_vgs(vgs, vgs_t)
    for i in range(count):
        part = mm(left, weights[i][...], (1, 1)) * gain[i]
        out_m[i] = part[:tokens].astype(BF16)
        out_t[i] = part[tokens:].astype(BF16)


def first_terms(vgs, vgs_t, gain, weights):
    count = len(weights)
    out = sds((count, vgs.shape[0], weights[0].shape[0]), BF16)
    return pl.pallas_call(
        functools.partial(first_kernel, count=count),
        out_shape=[out, out],
        compiler_params=params(),
        cost_estimate=SMALL,
        name="first_terms",
    )(vgs, vgs_t, gain, *weights)


def local_kernel(*refs, parts, shares, width):
    mine, theirs, vgs, vgs_t, gain, inverse, own, got = refs[:8]
    weights, outs = refs[8 : 8 + len(parts)], refs[8 + len(parts) :]
    blocks = sum(shares, [])
    rows = mine.shape[2]
    tokens, wide = vgs.shape
    one, two, three = (slice(wide + i * HD, wide + (i + 1) * HD) for i in range(3))
    inv_m, inv_t = inverse[...], got[:, three]
    c_m = inv_m * inv_m * (own[:, one] + got[:, two]) / width
    c_t = inv_t * inv_t * (own[:, two] + got[:, one]) / width
    coarse = c_m.astype(BF16)
    fine = (c_m - coarse.astype(F32)).astype(BF16)
    lane = lax.broadcasted_iota(jnp.int32, c_m.shape, 1)
    outs[0][:, len(blocks) * rows :] = jnp.where(lane < HD // 2, coarse.astype(F32), fine.astype(F32)).astype(BF16)
    c_m = jnp.concatenate([c_m] * (rows // HD), axis=1)
    c_t = jnp.concatenate([c_t] * (rows // HD), axis=1)
    left = both_vgs(vgs, vgs_t)
    for part, w in zip(parts, weights, strict=True):
        r, at = part[0], span(part, rows)
        n = blocks.index(r)
        to = slice(n * rows + at.start, n * rows + at.stop)
        g = gain[r][:, at]
        over = 1.0 / g
        product = mm(left, w[...], (1, 1))
        h_m, h_t = features(mine, part).astype(F32), features(theirs, part).astype(F32)
        outs[0][:, to] = (product[:tokens] * g - h_m * over * c_m[:, at]).astype(BF16)
        outs[1][:, to] = (product[tokens:] * g - h_t * over * c_t[:, at]).astype(BF16)


def local_grads(mine, theirs, vgs, vgs_t, gain, inverse, own, got, shares, parts, weights, width):
    tokens, rows = mine.shape[1:]
    wide = sum(len(share) for share in shares) * rows
    out = [sds((tokens, wide + HD), BF16), sds((tokens, wide), BF16)]
    return pl.pallas_call(
        functools.partial(local_kernel, parts=parts, shares=shares, width=width),
        out_shape=out,
        compiler_params=params(),
        cost_estimate=SMALL,
        name="local_grad",
    )(mine, theirs, vgs, vgs_t, gain, inverse, own, got, *weights)


def weight_kernel(*refs, part):
    mine, theirs, vgs, vgs_t = refs[:4]
    out = refs[-1]
    total = mm(pair(mine, theirs, part), both_vgs(vgs, vgs_t), (0, 0))
    rows = total.shape[0]
    for side, arrived in enumerate(refs[4:-1]):
        if arrived is None:
            continue
        if arrived.shape[0] == rows:
            total = total + arrived[...].astype(F32)
        elif side == 0:
            total = jnp.concatenate([total[: rows // 2] + arrived[...].astype(F32), total[rows // 2 :]], axis=0)
        else:
            total = jnp.concatenate([total[: rows // 2], total[rows // 2 :] + arrived[...].astype(F32)], axis=0)
    out[...] = total.astype(BF16)


def weight_step(mine, theirs, vgs, vgs_t, part, from_behind=None, from_ahead=None):
    at = span(part, mine.shape[2])

    def kernel(*refs):
        refs = list(refs)
        if from_behind is None:
            refs.insert(4, None)
        if from_ahead is None:
            refs.insert(5, None)
        weight_kernel(*refs, part=part)

    arrived = [x for x in (from_behind, from_ahead) if x is not None]
    return pl.pallas_call(
        kernel,
        out_shape=sds((at.stop - at.start, vgs.shape[1]), BF16),
        compiler_params=params(),
        cost_estimate=SMALL,
        name="weight_step",
    )(mine, theirs, vgs, vgs_t, *arrived)


def weight_last_kernel(mine, theirs, vgs, vgs_t, f, b, out, held, sem):
    right = both_vgs(vgs, vgs_t)
    half = f.shape[0] // 2
    copies = []
    for side in range(2):
        at = slice(side * half, (side + 1) * half)
        total = mm(pair(mine, theirs, (0, side)), right, (0, 0))
        held[at, :] = (total + f[at, :].astype(F32) + b[at, :].astype(F32)).astype(BF16)
        copies.append(pltpu.make_async_copy(held.at[at, :], out.at[at, :], sem.at[side]))
        copies[-1].start()
    for copy in copies:
        copy.wait()


def weight_last(mine, theirs, vgs, vgs_t, f, b):
    return pl.pallas_call(
        weight_last_kernel,
        out_specs=pl.BlockSpec(memory_space=pl.ANY),
        out_shape=sds(f.shape, BF16),
        scratch_shapes=[pltpu.VMEM(f.shape, BF16), pltpu.SemaphoreType.DMA((2,))],
        compiler_params=params(),
        cost_estimate=SMALL,
        name="weight_last",
    )(mine, theirs, vgs, vgs_t, f, b)


def copies_of(pieces, shares, where, out, sem, first, rows):
    copies = []
    for piece, blocks in zip(pieces, shares, strict=True):
        for j, r in enumerate(blocks):
            column = pl.multiple_of(where[first + r] * rows, rows)
            source, target = piece.at[:, j * rows : (j + 1) * rows], out.at[:, pl.ds(column, rows)]
            copies.append(pltpu.make_async_copy(source, target, sem.at[len(copies)]))
    return copies


def early_kernel(where, pin, ones, twos, raw_m, raw_t, second, *refs, soon, shares, chips, rows):
    pieces, (out, done, sem, sems) = refs[:-4], refs[-4:]
    copies = copies_of(pieces, shares, where, out, sem, 1, rows)
    for copy in copies:
        copy.start()
    c = second[...].astype(F32)
    c = c + pltpu.roll(c, HD // 2, 1)
    c = jnp.concatenate([c] * (rows // HD), axis=1)
    for side, (terms, raw) in enumerate(((ones, raw_m), (twos, raw_t))):
        for i, r in enumerate(soon):
            done[side, i] = (terms[i].astype(F32) - raw[i].astype(F32) * c).astype(BF16)
            column = pl.multiple_of(where[1 + side * chips + r] * rows, rows)
            copies.append(pltpu.make_async_copy(done.at[side, i], out.at[:, pl.ds(column, rows)], sems.at[side, i]))
            copies[-1].start()
    for copy in copies:
        copy.wait()


def early_blocks(where, pin, ones, twos, raw_m, raw_t, pieces, soon, shares, chips, width):
    _, tokens, rows = ones.shape
    somewhere = pl.BlockSpec(memory_space=pl.ANY)
    return pl.pallas_call(
        functools.partial(early_kernel, soon=soon, shares=shares, chips=chips, rows=rows),
        grid=(1,),
        in_specs=[
            pl.BlockSpec(memory_space=pltpu.SMEM),
            somewhere,
            pl.BlockSpec(ones.shape, lambda i: (0, 0, 0)),
            pl.BlockSpec(twos.shape, lambda i: (0, 0, 0)),
            pl.BlockSpec(ones.shape, lambda i: (0, 0, 0)),
            pl.BlockSpec(ones.shape, lambda i: (0, 0, 0)),
            pl.BlockSpec((tokens, HD), lambda i: (0, len(shares[0]) * rows // HD)),
        ]
        + [somewhere] * len(pieces),
        out_specs=somewhere,
        out_shape=sds((tokens, width), BF16),
        scratch_shapes=[
            pltpu.VMEM((2, *ones.shape), BF16),
            pltpu.SemaphoreType.DMA((sum(len(x) for x in shares),)),
            pltpu.SemaphoreType.DMA((2, len(soon))),
        ],
        compiler_params=params(),
        cost_estimate=SMALL,
        name="early_blocks",
    )(where, pin, ones, twos, raw_m, raw_t, pieces[0], *pieces)


def join_kernel(where, base, *refs, shares, chips, rows):
    pieces, (out, sem) = refs[:-2], refs[-2:]
    copies = copies_of(pieces, shares, where, out, sem, 1 + chips, rows)
    for copy in copies:
        copy.start()
    for copy in copies:
        copy.wait()


def join(where, base, pieces, shares, chips, rows):
    somewhere = pl.BlockSpec(memory_space=pl.ANY)
    return pl.pallas_call(
        functools.partial(join_kernel, shares=shares, chips=chips, rows=rows),
        in_specs=[pl.BlockSpec(memory_space=pltpu.SMEM)] + [somewhere] * (1 + len(pieces)),
        out_specs=somewhere,
        out_shape=sds(base.shape, BF16),
        input_output_aliases={1: 0},
        scratch_shapes=[pltpu.SemaphoreType.DMA((sum(len(x) for x in shares),))],
        compiler_params=params(),
        cost_estimate=SMALL,
        name="join",
    )(where, base, *pieces)


def fence_kernel(x, out):
    out[...] = x[...]


def fence(x, us):
    return pl.pallas_call(
        fence_kernel,
        out_shape=sds(x.shape, x.dtype),
        compiler_params=params(),
        cost_estimate=cost(us),
        name="fence",
    )(x)


def last_layer(layer_counts, layers):
    sections, mine = lax.axis_size("section"), lax.axis_index("section")
    own = layer_counts[0]
    total = own
    if sections > 2:
        reach = 1
        while reach < sections:
            route = [(i, i + reach) for i in range(sections - reach)]
            total = total + lax.ppermute(total, "section", route)
            reach *= 2
    return jnp.where(mine == sections - 1, layers, total) - 1


def shards(hidden, gain_table, layer_counts, positions, queries, keys, value_weight, out_grad):
    tokens_in, weight = hidden[0], value_weight[0]
    tokens, width = tokens_in.shape
    rows = weight.shape[0]
    sections = lax.axis_size("section")
    devices = lax.axis_size("dp")
    chips = devices // 2
    ring = list(range(0, chips, 2)) + list(range(1, chips, 2))[::-1]
    place_of = [ring.index(c) for c in range(chips)]
    me = lax.axis_index("dp")
    chip, core = me // 2, me % 2
    place = jnp.where(chip % 2 == 0, chip // 2, chips - 1 - chip // 2)
    spots = (place + jnp.arange(chips, dtype=jnp.int32)) % chips
    order = 2 * jnp.where(spots < (chips + 1) // 2, 2 * spots, 2 * (chips - 1 - spots) + 1)

    def hop(d, by):
        return 2 * ring[(place_of[d // 2] + by) % chips] + d % 2

    forth = [(d, hop(d, 1)) for d in range(devices)]
    back = [(d, hop(d, -1)) for d in range(devices)]
    swap = [(d, d ^ 1) for d in range(devices)]
    down = [(s * devices + d, (s - 1) * devices + d) for s in range(1, sections) for d in range(devices)]
    cross = [(s * devices + d, (s - 1) * devices + (d ^ 1)) for s in range(1, sections) for d in range(devices)]

    half = chips // 2
    low, high = slice(0, rows // 2), slice(rows // 2, rows)
    soon = [0, 1, chips - 1]
    later = [[r for r in range(chips) if r not in soon]]

    def ahead(x):
        return lax.ppermute(x, "dp", forth)

    def behind(x):
        return lax.ppermute(x, "dp", back)

    def swapped(x):
        return lax.ppermute(x, "dp", swap)

    def sent_down(x):
        return lax.ppermute(x, ("section", "dp"), down)

    def sent_across(x):
        return lax.ppermute(x, ("section", "dp"), cross)

    token = []

    def after(x):
        x = lax.optimization_barrier((x, *token))[0] if token else x
        token[:] = [x]
        return x

    def then(*results):
        token[:] = [results[0]]
        return results if len(results) > 1 else results[0]

    pin = [jnp.zeros((8, HD), F32)]

    def hold(us):
        pin[0] = then(fence(after(pin[0]), us))

    def parts_of(some):
        return [part for part in held if part[0] in some]

    def weights(parts):
        return [held[part] for part in parts]

    held = {(0, None): weight}
    moving = {(chips - 1, None): ahead(weight), (1, None): behind(weight)}

    def gather_next(step, side):
        for r, back_r, half_side, move in ((chips - step, chips - step + 1, side, ahead), (step, step - 1, 1 - side, behind)):
            if step == 2:
                source = held[back_r, None][high if half_side else low]
            else:
                source = held[back_r, half_side]
            moving[r, half_side] = move(source)

    def gather_here(step, side):
        for key in ((chips - step, side), (step, 1 - side)):
            held[key] = after(moving.pop(key))

    last = last_layer(layer_counts, gain_table.shape[0])
    where = jnp.concatenate([last[None], order + core, order + 1 - core]).astype(jnp.int32)
    cosine, sine = rope_tables(positions[0])
    raw_m, raw_t = then(*pick(where, tokens_in, soon, chips, rows))
    raw_m = sent_down(raw_m)
    mine, send, gain, inverse = then(*prep(after(where), tokens_in, gain_table, chips, rows))
    theirs = swapped(send)
    probs, q_rot, k_rot, vgs = then(
        *attention_probs(queries[0], keys[0], out_grad[0], cosine, sine, after(inverse))
    )
    vgs_t = swapped(vgs)
    hold(H[0])
    for key in ((chips - 1, None), (1, None)):
        held[key] = after(moving.pop(key))
    gather_next(2, 0)
    theirs, vgs_t = after(theirs), after(vgs_t)
    soon_gain = jnp.concatenate([gain[r : r + 1] for r in soon], axis=0)
    parts = parts_of(soon)
    one, two = then(*first_terms(after(vgs), vgs_t, soon_gain, [held[r, None] for r in soon]))
    late = {r: after(held[r, None]) for r in (chips - 1, 1)}
    moving[chips - 2, 1] = ahead(late[chips - 1][high])
    moving[2, 0] = behind(late[1][low])
    raw_m = after(raw_m)
    one = sent_down(after(one))
    total = then(values_sum(after(mine), theirs, parts, weights(parts)))
    hold(H[1])
    for step in range(2, half):
        gather_here(step, 0)
        if step + 1 <= half:
            gather_next(step + 1, 0)
        hold(H[2])
        gather_here(step, 1)
        if step + 1 < half:
            gather_next(step + 1, 1)
        if step == 2:
            one = after(one)
            two = sent_across(after(two))
        if step < half - 1:
            parts = parts_of([step, chips - step])
            total = then(values_sum(after(mine), theirs, parts, weights(parts), (total,)))
            hold(H[3])

    def weight_part(part, *arrived):
        return then(weight_step(after(mine), theirs, vgs, vgs_t, part, *arrived))

    f = ahead(weight_part((half, 0)))
    b = behind(weight_part((half, 1)))
    two = after(two)
    raw_t = sent_down(after(raw_t))
    hold(H[4])
    parts = parts_of([half - 1, half + 1])
    total = then(values_sum(after(mine), theirs, parts, weights(parts), (total,)))
    for key in ((half, 0), (half, 1)):
        held[key] = after(moving.pop(key))
    parts = parts_of([half])
    u_mine, packed = values_sum(after(mine), theirs, parts, weights(parts), (total,), (vgs, vgs_t, inverse))
    got = swapped(then(packed))

    def weight_turn(r, f, b):
        f = ahead(weight_part((r, None), after(f)))
        b = behind(weight_part((chips - r, None), None, after(b)))
        return f, b

    if half > 2:
        f, b = weight_turn(half - 1, f, b)
    hold(H[5])
    got = after(got)
    parts = parts_of(sum(later, []))
    m, t = then(
        *local_grads(
            mine, theirs, after(vgs), vgs_t, gain, inverse, packed, got, later, parts, weights(parts), width
        )
    )
    m, t = sent_down(m), sent_across(t)
    query_grad, key_grad = then(
        *attention_back(probs, q_rot, k_rot, out_grad[0], after(u_mine), got, cosine, sine, inverse)
    )
    hold(H[6])
    for r in range(half - 2, 0, -1):
        f, b = weight_turn(r, f, b)
        if r == 2:
            raw_t = after(raw_t)
        hold(H[7])
    upstream = then(
        early_blocks(where, pin[0], one, two, raw_m, raw_t, [after(m)], soon, [sum(later, [])], chips, width)
    )
    t = after(t)
    upstream = then(join(where, after(upstream), [t], [sum(later, [])], chips, rows))
    f, b = after(f), after(b)
    weight_grad = weight_last(mine, theirs, vgs, vgs_t, f, b)
    return (query_grad[None], key_grad[None], weight_grad[None], upstream[None])


def solution(mesh):
    split = P("section", "dp", None)
    in_specs = (split, P(), P("section"), P("section", "dp"), split, split, split, split)
    out_specs = (split,) * 4
    return jax.shard_map(shards, mesh=mesh, in_specs=in_specs, out_specs=out_specs, check_vma=False)
```

```python
import functools
import math

import jax
import jax.numpy as jnp
from jax import lax
from jax.experimental import pallas as pl
from jax.experimental.pallas import tpu as pltpu
from jax.sharding import PartitionSpec as P

HQ = 32
HK = 4
HD = 128
SHARE = HQ // HK
EPS = 1e-05
F32 = jnp.float32
BF16 = jnp.bfloat16
VMEM_LIMIT = 20 * 1024 * 1024


def cost(us):
    return pl.CostEstimate(flops=int(us * 1e9) + 1, bytes_accessed=1024, transcendentals=0)


SMALL = cost(0.2)
H = [12.0, 9.0, 1.5, 1.5, 1.5, 6.0, 3.0, 6.0]


def params(**more):
    return pltpu.CompilerParams(vmem_limit_bytes=VMEM_LIMIT, **more)


def mm(a, b, contract):
    return lax.dot_general(a, b, ((contract[:1], contract[1:]), ((), ())), preferred_element_type=F32)


def sds(shape, dtype):
    return jax.ShapeDtypeStruct(shape, dtype)


def rope_tables(places):
    half = HD // 2
    steps = jnp.arange(half, dtype=F32)
    freq = jnp.exp(steps * (-2.0 * math.log(500000.0) / HD))
    angle = places.astype(F32)[:, None] * freq[None, :]
    cosine, sine = jnp.cos(angle), jnp.sin(angle)
    return jnp.concatenate([cosine, cosine], 1), jnp.concatenate([-sine, sine], 1)


def turn(x, cosine, sine):
    return x * cosine + pltpu.roll(x, HD // 2, 1) * sine


def turn_back(x, cosine, sine):
    return x * cosine - pltpu.roll(x, HD // 2, 1) * sine


def prep_kernel(
    where, mine_in, theirs_in, gain_m, gain_t, mine, theirs, gain_out, inverse, total, *, width
):
    step = pl.program_id(0)
    rows = lax.broadcasted_iota(jnp.int32, gain_m.shape, 0) == where[0]
    g_m = jnp.sum(jnp.where(rows, gain_m[...].astype(F32), 0.0), axis=0, keepdims=True)
    g_t = jnp.sum(jnp.where(rows, gain_t[...].astype(F32), 0.0), axis=0, keepdims=True)
    h_m = mine_in[...].astype(F32)
    h_t = theirs_in[...].astype(F32)
    mine[0] = (h_m * g_m).astype(BF16)
    theirs[0] = (h_t * g_t).astype(BF16)
    gain_out[0] = g_m
    part = jnp.sum(h_m * h_m + h_t * h_t, axis=1, keepdims=True)
    @pl.when(step == 0)
    def _():
        total[...] = jnp.broadcast_to(part, total.shape)

    @pl.when(step > 0)
    def _():
        total[...] += jnp.broadcast_to(part, total.shape)

    @pl.when(step == pl.num_programs(0) - 1)
    def _():
        inverse[...] = lax.rsqrt(total[...] / width + EPS)


def prep(where, hidden, gain_table, chips, rows):
    tokens, width = hidden.shape
    layers = gain_table.shape[0]
    mine = lambda r, where: (0, where[1 + r])
    theirs = lambda r, where: (0, where[1 + chips + r])
    return pl.pallas_call(
        functools.partial(prep_kernel, width=width),
        grid_spec=pltpu.PrefetchScalarGridSpec(
            num_scalar_prefetch=1,
            grid=(chips,),
            in_specs=[
                pl.BlockSpec((tokens, rows), mine),
                pl.BlockSpec((tokens, rows), theirs),
                pl.BlockSpec((layers, rows), mine),
                pl.BlockSpec((layers, rows), theirs),
            ],
            out_specs=[
                pl.BlockSpec((1, tokens, rows), lambda r, where: (r, 0, 0)),
                pl.BlockSpec((1, tokens, rows), lambda r, where: (r, 0, 0)),
                pl.BlockSpec((1, 1, rows), lambda r, where: (r, 0, 0)),
                pl.BlockSpec((tokens, HD), lambda r, where: (0, 0)),
            ],
            scratch_shapes=[pltpu.VMEM((tokens, HD), F32)],
        ),
        out_shape=[
            sds((chips, tokens, rows), BF16),
            sds((chips, tokens, rows), BF16),
            sds((chips, 1, rows), F32),
            sds((tokens, HD), F32),
        ],
        compiler_params=params(),
        cost_estimate=SMALL,
        name="prep",
    )(where, hidden, hidden, gain_table, gain_table)


def pick_kernel(where, hidden, out_m, out_t, sem, *, soon, chips):
    rows = out_m.shape[2]
    copies = []
    for side, out in enumerate((out_m, out_t)):
        for i, r in enumerate(soon):
            column = pl.multiple_of(where[1 + side * chips + r] * rows, rows)
            source = hidden.at[:, pl.ds(column, rows)]
            copies.append(pltpu.make_async_copy(source, out.at[i], sem.at[side, i]))
    for copy in copies:
        copy.start()
    for copy in copies:
        copy.wait()


def pick(where, hidden, soon, chips, rows):
    somewhere = pl.BlockSpec(memory_space=pl.ANY)
    return pl.pallas_call(
        functools.partial(pick_kernel, soon=soon, chips=chips),
        in_specs=[pl.BlockSpec(memory_space=pltpu.SMEM), somewhere],
        out_specs=[somewhere, somewhere],
        out_shape=[sds((len(soon), hidden.shape[0], rows), BF16)] * 2,
        scratch_shapes=[pltpu.SemaphoreType.DMA((2, len(soon)))],
        compiler_params=params(),
        cost_estimate=SMALL,
        name="pick",
    )(where, hidden)


def stacked(ref):
    return jnp.concatenate([ref[:, h * HD : (h + 1) * HD] for h in range(SHARE)], axis=0)


def probs_kernel(q_ref, k_ref, d_ref, cosine, sine, inverse, probs, q_out, k_out, vgs):
    cos, sin = cosine[...], sine[...]
    tokens = k_ref.shape[0]
    k_rot = turn(k_ref[...].astype(F32), cos, sin).astype(BF16)
    q_rot = jnp.concatenate(
        [turn(q_ref[:, h * HD : (h + 1) * HD].astype(F32), cos, sin).astype(BF16) for h in range(SHARE)],
        axis=0,
    )
    q_out[0] = q_rot
    k_out[0] = k_rot
    scores = mm(k_rot, q_rot, (1, 1)) * (HD**-0.5)
    key_at = lax.broadcasted_iota(jnp.int32, (tokens, tokens), 0)
    query_at = lax.broadcasted_iota(jnp.int32, (tokens, tokens), 1)
    seen = key_at <= query_at
    lows = []
    for h in range(SHARE):
        s = jnp.where(seen, scores[:, h * tokens : (h + 1) * tokens], -1e30)
        e = jnp.exp(s - jnp.max(s, axis=0, keepdims=True))
        p = e / jnp.sum(e, axis=0, keepdims=True)
        probs[0, :, h * tokens : (h + 1) * tokens] = p
        lows.append(p.astype(BF16))
    grad = mm(jnp.concatenate(lows, axis=1), stacked(d_ref), (1, 0))
    vgs[...] = (grad * inverse[...]).astype(BF16)


def attention_probs(queries, keys, out_grad, cosine, sine, inverse):
    tokens = queries.shape[0]
    group = pl.BlockSpec((tokens, SHARE * HD), lambda g: (0, g))
    head = pl.BlockSpec((tokens, HD), lambda g: (0, g))
    table = pl.BlockSpec((tokens, HD), lambda g: (0, 0))
    return pl.pallas_call(
        probs_kernel,
        grid=(HK,),
        in_specs=[group, head, group, table, table, table],
        out_specs=[
            pl.BlockSpec((1, tokens, SHARE * tokens), lambda g: (g, 0, 0)),
            pl.BlockSpec((1, SHARE * tokens, HD), lambda g: (g, 0, 0)),
            pl.BlockSpec((1, tokens, HD), lambda g: (g, 0, 0)),
            head,
        ],
        out_shape=[
            pltpu.HBM((HK, tokens, SHARE * tokens), F32),
            pltpu.HBM((HK, SHARE * tokens, HD), BF16),
            pltpu.HBM((HK, tokens, HD), BF16),
            sds((tokens, HK * HD), BF16),
        ],
        compiler_params=params(),
        cost_estimate=SMALL,
        name="probs",
    )(queries, keys, out_grad, cosine, sine, inverse)


def back_kernel(probs, q_rot, k_rot, d_ref, u_one, u_two, cosine, sine, inverse, dq, dk):
    cos, sin = cosine[...], sine[...]
    tokens = k_rot.shape[1]
    values = ((u_one[...] + u_two[...]) * inverse[...]).astype(BF16)
    d_probs = mm(values, stacked(d_ref), (1, 1))
    p = probs[0]
    delta = jnp.sum(p.astype(BF16).astype(F32) * d_probs, axis=0, keepdims=True)
    d_scores = (p * (d_probs - delta) * (HD**-0.5)).astype(BF16)
    dk[...] = turn_back(mm(d_scores, q_rot[0], (1, 0)), cos, sin).astype(BF16)
    key = k_rot[0]
    for h in range(SHARE):
        part = mm(d_scores[:, h * tokens : (h + 1) * tokens], key, (0, 0))
        dq[:, h * HD : (h + 1) * HD] = turn_back(part, cos, sin).astype(BF16)


def attention_back(probs, q_rot, k_rot, out_grad, u_one, u_two, cosine, sine, inverse):
    tokens = out_grad.shape[0]
    group = pl.BlockSpec((tokens, SHARE * HD), lambda g: (0, g))
    head = pl.BlockSpec((tokens, HD), lambda g: (0, g))
    table = pl.BlockSpec((tokens, HD), lambda g: (0, 0))
    return pl.pallas_call(
        back_kernel,
        grid=(HK,),
        in_specs=[
            pl.BlockSpec((1, tokens, SHARE * tokens), lambda g: (g, 0, 0)),
            pl.BlockSpec((1, SHARE * tokens, HD), lambda g: (g, 0, 0)),
            pl.BlockSpec((1, tokens, HD), lambda g: (g, 0, 0)),
            group,
            head,
            head,
            table,
            table,
            table,
        ],
        out_specs=[group, head],
        out_shape=[sds((tokens, HQ * HD), BF16), sds((tokens, HK * HD), BF16)],
        compiler_params=params(),
        cost_estimate=SMALL,
        name="back",
    )(probs, q_rot, k_rot, out_grad, u_one, u_two, cosine, sine, inverse)


def span(part, rows):
    side = part[1]
    return slice(0, rows) if side is None else slice(side * rows // 2, (side + 1) * rows // 2)


def features(ref, part):
    return ref[part[0]][:, span(part, ref.shape[2])]


def both_vgs(vgs, vgs_t):
    return jnp.concatenate([vgs[...], vgs_t[...]], axis=0)


def pair(mine, theirs, part):
    return jnp.concatenate([features(mine, part), features(theirs, part)], axis=0)


def values_kernel(*refs, parts, first, last):
    mine, theirs = refs[0], refs[1]
    weights, rest = refs[2 : 2 + len(parts)], refs[2 + len(parts) :]
    tokens = mine.shape[1]
    acc = None
    if not first:
        acc, rest = rest[0][...], rest[1:]
    for part, w in zip(parts, weights, strict=True):
        product = mm(pair(mine, theirs, part), w[...], (1, 0))
        acc = product if acc is None else acc + product
    if not last:
        rest[0][...] = acc
        return
    vgs, vgs_t, inverse, u_mine, packed = rest
    vgs = both_vgs(vgs, vgs_t).astype(F32)
    wide = acc.shape[1]
    u_mine[...] = acc[:tokens]
    packed[:, :wide] = acc[tokens:]
    dot_m = jnp.sum(acc[:tokens] * vgs[:tokens], axis=1, keepdims=True)
    dot_t = jnp.sum(acc[tokens:] * vgs[tokens:], axis=1, keepdims=True)
    packed[:, wide : wide + HD] = jnp.broadcast_to(dot_m, (tokens, HD))
    packed[:, wide + HD : wide + 2 * HD] = jnp.broadcast_to(dot_t, (tokens, HD))
    packed[:, wide + 2 * HD :] = inverse[...]


def values_sum(mine, theirs, parts, weights, before=(), final=()):
    tokens, wide = mine.shape[1], weights[0].shape[1]
    if final:
        out = [sds((tokens, wide), F32), sds((tokens, wide + 3 * HD), F32)]
    else:
        out = sds((2 * tokens, wide), F32)
    return pl.pallas_call(
        functools.partial(values_kernel, parts=parts, first=not before, last=bool(final)),
        out_shape=out,
        compiler_params=params(),
        cost_estimate=SMALL,
        name="values",
    )(mine, theirs, *weights, *before, *final)


def first_kernel(*refs, count):
    vgs, vgs_t, gain = refs[:3]
    weights, (out_m, out_t) = refs[3 : 3 + count], refs[3 + count :]
    tokens = vgs.shape[0]
    left = both_vgs(vgs, vgs_t)
    for i in range(count):
        part = mm(left, weights[i][...], (1, 1)) * gain[i]
        out_m[i] = part[:tokens].astype(BF16)
        out_t[i] = part[tokens:].astype(BF16)


def first_terms(vgs, vgs_t, gain, weights):
    count = len(weights)
    out = sds((count, vgs.shape[0], weights[0].shape[0]), BF16)
    return pl.pallas_call(
        functools.partial(first_kernel, count=count),
        out_shape=[out, out],
        compiler_params=params(),
        cost_estimate=SMALL,
        name="first_terms",
    )(vgs, vgs_t, gain, *weights)


def local_kernel(*refs, parts, shares, width):
    mine, theirs, vgs, vgs_t, gain, inverse, own, got = refs[:8]
    weights, outs = refs[8 : 8 + len(parts)], refs[8 + len(parts) :]
    blocks = sum(shares, [])
    rows = mine.shape[2]
    tokens, wide = vgs.shape
    one, two, three = (slice(wide + i * HD, wide + (i + 1) * HD) for i in range(3))
    inv_m, inv_t = inverse[...], got[:, three]
    c_m = inv_m * inv_m * (own[:, one] + got[:, two]) / width
    c_t = inv_t * inv_t * (own[:, two] + got[:, one]) / width
    coarse = c_m.astype(BF16)
    fine = (c_m - coarse.astype(F32)).astype(BF16)
    lane = lax.broadcasted_iota(jnp.int32, c_m.shape, 1)
    outs[0][:, len(blocks) * rows :] = jnp.where(lane < HD // 2, coarse.astype(F32), fine.astype(F32)).astype(BF16)
    c_m = jnp.concatenate([c_m] * (rows // HD), axis=1)
    c_t = jnp.concatenate([c_t] * (rows // HD), axis=1)
    left = both_vgs(vgs, vgs_t)
    for part, w in zip(parts, weights, strict=True):
        r, at = part[0], span(part, rows)
        n = blocks.index(r)
        to = slice(n * rows + at.start, n * rows + at.stop)
        g = gain[r][:, at]
        over = 1.0 / g
        product = mm(left, w[...], (1, 1))
        h_m, h_t = features(mine, part).astype(F32), features(theirs, part).astype(F32)
        outs[0][:, to] = (product[:tokens] * g - h_m * over * c_m[:, at]).astype(BF16)
        outs[1][:, to] = (product[tokens:] * g - h_t * over * c_t[:, at]).astype(BF16)


def local_grads(mine, theirs, vgs, vgs_t, gain, inverse, own, got, shares, parts, weights, width):
    tokens, rows = mine.shape[1:]
    wide = sum(len(share) for share in shares) * rows
    out = [sds((tokens, wide + HD), BF16), sds((tokens, wide), BF16)]
    return pl.pallas_call(
        functools.partial(local_kernel, parts=parts, shares=shares, width=width),
        out_shape=out,
        compiler_params=params(),
        cost_estimate=SMALL,
        name="local_grad",
    )(mine, theirs, vgs, vgs_t, gain, inverse, own, got, *weights)


def weight_kernel(*refs, part):
    mine, theirs, vgs, vgs_t = refs[:4]
    out = refs[-1]
    total = mm(pair(mine, theirs, part), both_vgs(vgs, vgs_t), (0, 0))
    rows = total.shape[0]
    for side, arrived in enumerate(refs[4:-1]):
        if arrived is None:
            continue
        if arrived.shape[0] == rows:
            total = total + arrived[...].astype(F32)
        elif side == 0:
            total = jnp.concatenate([total[: rows // 2] + arrived[...].astype(F32), total[rows // 2 :]], axis=0)
        else:
            total = jnp.concatenate([total[: rows // 2], total[rows // 2 :] + arrived[...].astype(F32)], axis=0)
    out[...] = total.astype(BF16)


def weight_step(mine, theirs, vgs, vgs_t, part, from_behind=None, from_ahead=None):
    at = span(part, mine.shape[2])

    def kernel(*refs):
        refs = list(refs)
        if from_behind is None:
            refs.insert(4, None)
        if from_ahead is None:
            refs.insert(5, None)
        weight_kernel(*refs, part=part)

    arrived = [x for x in (from_behind, from_ahead) if x is not None]
    return pl.pallas_call(
        kernel,
        out_shape=sds((at.stop - at.start, vgs.shape[1]), BF16),
        compiler_params=params(),
        cost_estimate=SMALL,
        name="weight_step",
    )(mine, theirs, vgs, vgs_t, *arrived)


def weight_both_kernel(*refs, parts):
    mine, theirs, vgs, vgs_t = refs[:4]
    arrived, outs = refs[4:-2], refs[-2:]
    right = both_vgs(vgs, vgs_t)
    for i, (part, out) in enumerate(zip(parts, outs, strict=True)):
        total = mm(pair(mine, theirs, part), right, (0, 0))
        rows = total.shape[0]
        if arrived:
            more = arrived[i][...].astype(F32)
            if more.shape[0] == rows:
                total = total + more
            elif i == 0:
                total = jnp.concatenate([total[: rows // 2] + more, total[rows // 2 :]], axis=0)
            else:
                total = jnp.concatenate([total[: rows // 2], total[rows // 2 :] + more], axis=0)
        out[...] = total.astype(BF16)


def weight_both(mine, theirs, vgs, vgs_t, parts, arrived):
    ats = [span(part, mine.shape[2]) for part in parts]
    return pl.pallas_call(
        functools.partial(weight_both_kernel, parts=parts),
        out_shape=[sds((at.stop - at.start, vgs.shape[1]), BF16) for at in ats],
        compiler_params=params(),
        cost_estimate=SMALL,
        name="weight_both",
    )(mine, theirs, vgs, vgs_t, *arrived)


def weight_last_kernel(mine, theirs, vgs, vgs_t, f, b, out, held, sem):
    right = both_vgs(vgs, vgs_t)
    half = f.shape[0] // 2
    copies = []
    for side in range(2):
        at = slice(side * half, (side + 1) * half)
        total = mm(pair(mine, theirs, (0, side)), right, (0, 0))
        held[at, :] = (total + f[at, :].astype(F32) + b[at, :].astype(F32)).astype(BF16)
        copies.append(pltpu.make_async_copy(held.at[at, :], out.at[at, :], sem.at[side]))
        copies[-1].start()
    for copy in copies:
        copy.wait()


def weight_last(mine, theirs, vgs, vgs_t, f, b):
    return pl.pallas_call(
        weight_last_kernel,
        out_specs=pl.BlockSpec(memory_space=pl.ANY),
        out_shape=sds(f.shape, BF16),
        scratch_shapes=[pltpu.VMEM(f.shape, BF16), pltpu.SemaphoreType.DMA((2,))],
        compiler_params=params(),
        cost_estimate=SMALL,
        name="weight_last",
    )(mine, theirs, vgs, vgs_t, f, b)


def copies_of(pieces, shares, where, out, sem, first, rows):
    copies = []
    for piece, blocks in zip(pieces, shares, strict=True):
        for j, r in enumerate(blocks):
            column = pl.multiple_of(where[first + r] * rows, rows)
            source, target = piece.at[:, j * rows : (j + 1) * rows], out.at[:, pl.ds(column, rows)]
            copies.append(pltpu.make_async_copy(source, target, sem.at[len(copies)]))
    return copies


def early_kernel(where, pin, ones, twos, raw_m, raw_t, second, *refs, soon, shares, chips, rows):
    pieces, (out, done, sem, sems) = refs[:-4], refs[-4:]
    copies = copies_of(pieces, shares, where, out, sem, 1, rows)
    for copy in copies:
        copy.start()
    c = second[...].astype(F32)
    c = c + pltpu.roll(c, HD // 2, 1)
    c = jnp.concatenate([c] * (rows // HD), axis=1)
    for side, (terms, raw) in enumerate(((ones, raw_m), (twos, raw_t))):
        for i, r in enumerate(soon):
            done[side, i] = (terms[i].astype(F32) - raw[i].astype(F32) * c).astype(BF16)
            column = pl.multiple_of(where[1 + side * chips + r] * rows, rows)
            copies.append(pltpu.make_async_copy(done.at[side, i], out.at[:, pl.ds(column, rows)], sems.at[side, i]))
            copies[-1].start()
    for copy in copies:
        copy.wait()


def early_blocks(where, pin, ones, twos, raw_m, raw_t, pieces, soon, shares, chips, width):
    _, tokens, rows = ones.shape
    somewhere = pl.BlockSpec(memory_space=pl.ANY)
    return pl.pallas_call(
        functools.partial(early_kernel, soon=soon, shares=shares, chips=chips, rows=rows),
        grid=(1,),
        in_specs=[
            pl.BlockSpec(memory_space=pltpu.SMEM),
            somewhere,
            pl.BlockSpec(ones.shape, lambda i: (0, 0, 0)),
            pl.BlockSpec(twos.shape, lambda i: (0, 0, 0)),
            pl.BlockSpec(ones.shape, lambda i: (0, 0, 0)),
            pl.BlockSpec(ones.shape, lambda i: (0, 0, 0)),
            pl.BlockSpec((tokens, HD), lambda i: (0, len(shares[0]) * rows // HD)),
        ]
        + [somewhere] * len(pieces),
        out_specs=somewhere,
        out_shape=sds((tokens, width), BF16),
        scratch_shapes=[
            pltpu.VMEM((2, *ones.shape), BF16),
            pltpu.SemaphoreType.DMA((sum(len(x) for x in shares),)),
            pltpu.SemaphoreType.DMA((2, len(soon))),
        ],
        compiler_params=params(),
        cost_estimate=SMALL,
        name="early_blocks",
    )(where, pin, ones, twos, raw_m, raw_t, pieces[0], *pieces)


def join_kernel(where, base, *refs, shares, chips, rows):
    pieces, (out, sem) = refs[:-2], refs[-2:]
    copies = copies_of(pieces, shares, where, out, sem, 1 + chips, rows)
    for copy in copies:
        copy.start()
    for copy in copies:
        copy.wait()


def join(where, base, pieces, shares, chips, rows):
    somewhere = pl.BlockSpec(memory_space=pl.ANY)
    return pl.pallas_call(
        functools.partial(join_kernel, shares=shares, chips=chips, rows=rows),
        in_specs=[pl.BlockSpec(memory_space=pltpu.SMEM)] + [somewhere] * (1 + len(pieces)),
        out_specs=somewhere,
        out_shape=sds(base.shape, BF16),
        input_output_aliases={1: 0},
        scratch_shapes=[pltpu.SemaphoreType.DMA((sum(len(x) for x in shares),))],
        compiler_params=params(),
        cost_estimate=SMALL,
        name="join",
    )(where, base, *pieces)


def fence_kernel(x, out):
    out[...] = x[...]


def fence(x, us):
    return pl.pallas_call(
        fence_kernel,
        out_shape=sds(x.shape, x.dtype),
        compiler_params=params(),
        cost_estimate=cost(us),
        name="fence",
    )(x)


def last_layer(layer_counts, layers):
    sections, mine = lax.axis_size("section"), lax.axis_index("section")
    own = layer_counts[0]
    total = own
    if sections > 2:
        reach = 1
        while reach < sections:
            route = [(i, i + reach) for i in range(sections - reach)]
            total = total + lax.ppermute(total, "section", route)
            reach *= 2
    return jnp.where(mine == sections - 1, layers, total) - 1


def shards(hidden, gain_table, layer_counts, positions, queries, keys, value_weight, out_grad):
    tokens_in, weight = hidden[0], value_weight[0]
    tokens, width = tokens_in.shape
    rows = weight.shape[0]
    sections = lax.axis_size("section")
    devices = lax.axis_size("dp")
    chips = devices // 2
    ring = list(range(0, chips, 2)) + list(range(1, chips, 2))[::-1]
    place_of = [ring.index(c) for c in range(chips)]
    me = lax.axis_index("dp")
    chip, core = me // 2, me % 2
    place = jnp.where(chip % 2 == 0, chip // 2, chips - 1 - chip // 2)
    spots = (place + jnp.arange(chips, dtype=jnp.int32)) % chips
    order = 2 * jnp.where(spots < (chips + 1) // 2, 2 * spots, 2 * (chips - 1 - spots) + 1)

    def hop(d, by):
        return 2 * ring[(place_of[d // 2] + by) % chips] + d % 2

    forth = [(d, hop(d, 1)) for d in range(devices)]
    back = [(d, hop(d, -1)) for d in range(devices)]
    swap = [(d, d ^ 1) for d in range(devices)]
    down = [(s * devices + d, (s - 1) * devices + d) for s in range(1, sections) for d in range(devices)]
    cross = [(s * devices + d, (s - 1) * devices + (d ^ 1)) for s in range(1, sections) for d in range(devices)]

    half = chips // 2
    low, high = slice(0, rows // 2), slice(rows // 2, rows)
    soon = [0, 1, chips - 1]
    later = [[r for r in range(chips) if r not in soon]]

    def ahead(x):
        return lax.ppermute(x, "dp", forth)

    def behind(x):
        return lax.ppermute(x, "dp", back)

    def swapped(x):
        return lax.ppermute(x, "dp", swap)

    def sent_down(x):
        return lax.ppermute(x, ("section", "dp"), down)

    def sent_across(x):
        return lax.ppermute(x, ("section", "dp"), cross)

    token = []

    def after(x):
        x = lax.optimization_barrier((x, *token))[0] if token else x
        token[:] = [x]
        return x

    def then(*results):
        token[:] = [results[0]]
        return results if len(results) > 1 else results[0]

    pin = [jnp.zeros((8, HD), F32)]

    def hold(us):
        pin[0] = then(fence(after(pin[0]), us))

    def parts_of(some):
        return [part for part in held if part[0] in some]

    def weights(parts):
        return [held[part] for part in parts]

    held = {(0, None): weight}
    moving = {(chips - 1, None): ahead(weight), (1, None): behind(weight)}

    def gather_next(step, side):
        for r, back_r, half_side, move in ((chips - step, chips - step + 1, side, ahead), (step, step - 1, 1 - side, behind)):
            if step == 2:
                source = held[back_r, None][high if half_side else low]
            else:
                source = held[back_r, half_side]
            moving[r, half_side] = move(source)

    def gather_here(step, side):
        for key in ((chips - step, side), (step, 1 - side)):
            held[key] = after(moving.pop(key))

    last = last_layer(layer_counts, gain_table.shape[0])
    where = jnp.concatenate([last[None], order + core, order + 1 - core]).astype(jnp.int32)
    cosine, sine = rope_tables(positions[0])
    raw_m, raw_t = then(*pick(where, tokens_in, soon, chips, rows))
    raw_m = sent_down(raw_m)
    mine, send, gain, inverse = then(*prep(after(where), tokens_in, gain_table, chips, rows))
    theirs = swapped(send)
    probs, q_rot, k_rot, vgs = then(
        *attention_probs(queries[0], keys[0], out_grad[0], cosine, sine, after(inverse))
    )
    vgs_t = swapped(vgs)
    hold(H[0])
    for key in ((chips - 1, None), (1, None)):
        held[key] = after(moving.pop(key))
    gather_next(2, 0)
    theirs, vgs_t = after(theirs), after(vgs_t)
    soon_gain = jnp.concatenate([gain[r : r + 1] for r in soon], axis=0)
    parts = parts_of(soon)
    one, two = then(*first_terms(after(vgs), vgs_t, soon_gain, [held[r, None] for r in soon]))
    late = {r: after(held[r, None]) for r in (chips - 1, 1)}
    moving[chips - 2, 1] = ahead(late[chips - 1][high])
    moving[2, 0] = behind(late[1][low])
    raw_m = after(raw_m)
    one = sent_down(after(one))
    total = then(values_sum(after(mine), theirs, parts, weights(parts)))
    hold(H[1])
    for step in range(2, half):
        gather_here(step, 0)
        if step + 1 <= half:
            gather_next(step + 1, 0)
        hold(H[2])
        gather_here(step, 1)
        if step + 1 < half:
            gather_next(step + 1, 1)
        if step == 2:
            one = after(one)
            two = sent_across(after(two))
        if step < half - 1:
            parts = parts_of([step, chips - step])
            total = then(values_sum(after(mine), theirs, parts, weights(parts), (total,)))
            hold(H[3])

    def weight_parts(parts, *arrived):
        arrived = [after(x) for x in arrived]
        f, b = then(*weight_both(after(mine), theirs, vgs, vgs_t, parts, arrived))
        return ahead(f), behind(b)

    f, b = weight_parts(((half, 0), (half, 1)))
    two = after(two)
    raw_t = sent_down(after(raw_t))
    hold(H[4])
    parts = parts_of([half - 1, half + 1])
    total = then(values_sum(after(mine), theirs, parts, weights(parts), (total,)))
    for key in ((half, 0), (half, 1)):
        held[key] = after(moving.pop(key))
    parts = parts_of([half])
    u_mine, packed = values_sum(after(mine), theirs, parts, weights(parts), (total,), (vgs, vgs_t, inverse))
    got = swapped(then(packed))

    def weight_part(part, *arrived):
        return then(weight_step(after(mine), theirs, vgs, vgs_t, part, *arrived))

    def weight_turn(r, f, b):
        f = ahead(weight_part((r, None), after(f)))
        b = behind(weight_part((chips - r, None), None, after(b)))
        return f, b

    if half > 2:
        f, b = weight_parts(((half - 1, None), (half + 1, None)), f, b)
    hold(H[5])
    got = after(got)
    parts = parts_of(sum(later, []))
    m, t = then(
        *local_grads(
            mine, theirs, after(vgs), vgs_t, gain, inverse, packed, got, later, parts, weights(parts), width
        )
    )
    m, t = sent_down(m), sent_across(t)
    query_grad, key_grad = then(
        *attention_back(probs, q_rot, k_rot, out_grad[0], after(u_mine), got, cosine, sine, inverse)
    )
    hold(H[6])
    for r in range(half - 2, 0, -1):
        f, b = weight_turn(r, f, b)
        if r == 2:
            raw_t = after(raw_t)
        hold(H[7])
    upstream = then(
        early_blocks(where, pin[0], one, two, raw_m, raw_t, [after(m)], soon, [sum(later, [])], chips, width)
    )
    t = after(t)
    upstream = then(join(where, after(upstream), [t], [sum(later, [])], chips, rows))
    f, b = after(f), after(b)
    weight_grad = weight_last(mine, theirs, vgs, vgs_t, f, b)
    return (query_grad[None], key_grad[None], weight_grad[None], upstream[None])


def solution(mesh):
    split = P("section", "dp", None)
    in_specs = (split, P(), P("section"), P("section", "dp"), split, split, split, split)
    out_specs = (split,) * 4
    return jax.shard_map(shards, mesh=mesh, in_specs=in_specs, out_specs=out_specs, check_vma=False)
```

```python
import functools
import math

import jax
import jax.numpy as jnp
from jax import lax
from jax.experimental import pallas as pl
from jax.experimental.pallas import tpu as pltpu
from jax.sharding import PartitionSpec as P

HQ = 32
HK = 4
HD = 128
SHARE = HQ // HK
EPS = 1e-05
F32 = jnp.float32
BF16 = jnp.bfloat16
VMEM_LIMIT = 20 * 1024 * 1024


def cost(us):
    return pl.CostEstimate(flops=int(us * 1e9) + 1, bytes_accessed=1024, transcendentals=0)


SMALL = cost(0.2)
H = [5.0, 5.0, 1.5, 9.0, 0.3, 6.0, 6.0, 6.0]


def params(**more):
    return pltpu.CompilerParams(vmem_limit_bytes=VMEM_LIMIT, **more)


def mm(a, b, contract):
    return lax.dot_general(a, b, ((contract[:1], contract[1:]), ((), ())), preferred_element_type=F32)


def sds(shape, dtype):
    return jax.ShapeDtypeStruct(shape, dtype)


def rope_tables(places):
    half = HD // 2
    steps = jnp.arange(half, dtype=F32)
    freq = jnp.exp(steps * (-2.0 * math.log(500000.0) / HD))
    angle = places.astype(F32)[:, None] * freq[None, :]
    cosine, sine = jnp.cos(angle), jnp.sin(angle)
    return jnp.concatenate([cosine, cosine], 1), jnp.concatenate([-sine, sine], 1)


def turn(x, cosine, sine):
    return x * cosine + pltpu.roll(x, HD // 2, 1) * sine


def turn_back(x, cosine, sine):
    return x * cosine - pltpu.roll(x, HD // 2, 1) * sine


def prep_kernel(
    where, mine_in, theirs_in, gain_m, gain_t, mine, theirs, gain_out, inverse, total, *, width
):
    step = pl.program_id(0)
    rows = lax.broadcasted_iota(jnp.int32, gain_m.shape, 0) == where[0]
    g_m = jnp.sum(jnp.where(rows, gain_m[...].astype(F32), 0.0), axis=0, keepdims=True)
    g_t = jnp.sum(jnp.where(rows, gain_t[...].astype(F32), 0.0), axis=0, keepdims=True)
    h_m = mine_in[...].astype(F32)
    h_t = theirs_in[...].astype(F32)
    mine[0] = (h_m * g_m).astype(BF16)
    theirs[0] = (h_t * g_t).astype(BF16)
    gain_out[0] = g_m
    part = jnp.sum(h_m * h_m + h_t * h_t, axis=1, keepdims=True)
    @pl.when(step == 0)
    def _():
        total[...] = jnp.broadcast_to(part, total.shape)

    @pl.when(step > 0)
    def _():
        total[...] += jnp.broadcast_to(part, total.shape)

    @pl.when(step == pl.num_programs(0) - 1)
    def _():
        inverse[...] = lax.rsqrt(total[...] / width + EPS)


def prep(where, hidden, gain_table, chips, rows):
    tokens, width = hidden.shape
    layers = gain_table.shape[0]
    mine = lambda r, where: (0, where[1 + r])
    theirs = lambda r, where: (0, where[1 + chips + r])
    return pl.pallas_call(
        functools.partial(prep_kernel, width=width),
        grid_spec=pltpu.PrefetchScalarGridSpec(
            num_scalar_prefetch=1,
            grid=(chips,),
            in_specs=[
                pl.BlockSpec((tokens, rows), mine),
                pl.BlockSpec((tokens, rows), theirs),
                pl.BlockSpec((layers, rows), mine),
                pl.BlockSpec((layers, rows), theirs),
            ],
            out_specs=[
                pl.BlockSpec((1, tokens, rows), lambda r, where: (r, 0, 0)),
                pl.BlockSpec((1, tokens, rows), lambda r, where: (r, 0, 0)),
                pl.BlockSpec((1, 1, rows), lambda r, where: (r, 0, 0)),
                pl.BlockSpec((tokens, HD), lambda r, where: (0, 0)),
            ],
            scratch_shapes=[pltpu.VMEM((tokens, HD), F32)],
        ),
        out_shape=[
            sds((chips, tokens, rows), BF16),
            sds((chips, tokens, rows), BF16),
            sds((chips, 1, rows), F32),
            sds((tokens, HD), F32),
        ],
        compiler_params=params(),
        cost_estimate=SMALL,
        name="prep",
    )(where, hidden, hidden, gain_table, gain_table)


def pick_kernel(where, hidden, out_m, out_t, sem, *, soon, chips):
    rows = out_m.shape[2]
    copies = []
    for side, out in enumerate((out_m, out_t)):
        for i, r in enumerate(soon):
            column = pl.multiple_of(where[1 + side * chips + r] * rows, rows)
            source = hidden.at[:, pl.ds(column, rows)]
            copies.append(pltpu.make_async_copy(source, out.at[i], sem.at[side, i]))
    for copy in copies:
        copy.start()
    for copy in copies:
        copy.wait()


def pick(where, hidden, soon, chips, rows):
    somewhere = pl.BlockSpec(memory_space=pl.ANY)
    return pl.pallas_call(
        functools.partial(pick_kernel, soon=soon, chips=chips),
        in_specs=[pl.BlockSpec(memory_space=pltpu.SMEM), somewhere],
        out_specs=[somewhere, somewhere],
        out_shape=[sds((len(soon), hidden.shape[0], rows), BF16)] * 2,
        scratch_shapes=[pltpu.SemaphoreType.DMA((2, len(soon)))],
        compiler_params=params(),
        cost_estimate=SMALL,
        name="pick",
    )(where, hidden)


def stacked(ref):
    return jnp.concatenate([ref[:, h * HD : (h + 1) * HD] for h in range(SHARE)], axis=0)


def probs_kernel(q_ref, k_ref, d_ref, cosine, sine, inverse, probs, q_out, k_out, vgs):
    cos, sin = cosine[...], sine[...]
    tokens = k_ref.shape[0]
    k_rot = turn(k_ref[...].astype(F32), cos, sin).astype(BF16)
    q_rot = jnp.concatenate(
        [turn(q_ref[:, h * HD : (h + 1) * HD].astype(F32), cos, sin).astype(BF16) for h in range(SHARE)],
        axis=0,
    )
    q_out[0] = q_rot
    k_out[0] = k_rot
    scores = mm(k_rot, q_rot, (1, 1)) * (HD**-0.5)
    key_at = lax.broadcasted_iota(jnp.int32, (tokens, tokens), 0)
    query_at = lax.broadcasted_iota(jnp.int32, (tokens, tokens), 1)
    seen = key_at <= query_at
    lows = []
    for h in range(SHARE):
        s = jnp.where(seen, scores[:, h * tokens : (h + 1) * tokens], -1e30)
        e = jnp.exp(s - jnp.max(s, axis=0, keepdims=True))
        p = e / jnp.sum(e, axis=0, keepdims=True)
        probs[0, :, h * tokens : (h + 1) * tokens] = p
        lows.append(p.astype(BF16))
    grad = mm(jnp.concatenate(lows, axis=1), stacked(d_ref), (1, 0))
    vgs[...] = (grad * inverse[...]).astype(BF16)


def attention_probs(queries, keys, out_grad, cosine, sine, inverse):
    tokens = queries.shape[0]
    group = pl.BlockSpec((tokens, SHARE * HD), lambda g: (0, g))
    head = pl.BlockSpec((tokens, HD), lambda g: (0, g))
    table = pl.BlockSpec((tokens, HD), lambda g: (0, 0))
    return pl.pallas_call(
        probs_kernel,
        grid=(HK,),
        in_specs=[group, head, group, table, table, table],
        out_specs=[
            pl.BlockSpec((1, tokens, SHARE * tokens), lambda g: (g, 0, 0)),
            pl.BlockSpec((1, SHARE * tokens, HD), lambda g: (g, 0, 0)),
            pl.BlockSpec((1, tokens, HD), lambda g: (g, 0, 0)),
            head,
        ],
        out_shape=[
            pltpu.HBM((HK, tokens, SHARE * tokens), F32),
            pltpu.HBM((HK, SHARE * tokens, HD), BF16),
            pltpu.HBM((HK, tokens, HD), BF16),
            sds((tokens, HK * HD), BF16),
        ],
        compiler_params=params(),
        cost_estimate=SMALL,
        name="probs",
    )(queries, keys, out_grad, cosine, sine, inverse)


def back_kernel(probs, q_rot, k_rot, d_ref, u_one, u_two, cosine, sine, inverse, dq, dk):
    cos, sin = cosine[...], sine[...]
    tokens = k_rot.shape[1]
    values = ((u_one[...] + u_two[...]) * inverse[...]).astype(BF16)
    d_probs = mm(values, stacked(d_ref), (1, 1))
    p = probs[0]
    delta = jnp.sum(p.astype(BF16).astype(F32) * d_probs, axis=0, keepdims=True)
    d_scores = (p * (d_probs - delta) * (HD**-0.5)).astype(BF16)
    dk[...] = turn_back(mm(d_scores, q_rot[0], (1, 0)), cos, sin).astype(BF16)
    key = k_rot[0]
    for h in range(SHARE):
        part = mm(d_scores[:, h * tokens : (h + 1) * tokens], key, (0, 0))
        dq[:, h * HD : (h + 1) * HD] = turn_back(part, cos, sin).astype(BF16)


def attention_back(probs, q_rot, k_rot, out_grad, u_one, u_two, cosine, sine, inverse):
    tokens = out_grad.shape[0]
    group = pl.BlockSpec((tokens, SHARE * HD), lambda g: (0, g))
    head = pl.BlockSpec((tokens, HD), lambda g: (0, g))
    table = pl.BlockSpec((tokens, HD), lambda g: (0, 0))
    return pl.pallas_call(
        back_kernel,
        grid=(HK,),
        in_specs=[
            pl.BlockSpec((1, tokens, SHARE * tokens), lambda g: (g, 0, 0)),
            pl.BlockSpec((1, SHARE * tokens, HD), lambda g: (g, 0, 0)),
            pl.BlockSpec((1, tokens, HD), lambda g: (g, 0, 0)),
            group,
            head,
            head,
            table,
            table,
            table,
        ],
        out_specs=[group, head],
        out_shape=[sds((tokens, HQ * HD), BF16), sds((tokens, HK * HD), BF16)],
        compiler_params=params(),
        cost_estimate=SMALL,
        name="back",
    )(probs, q_rot, k_rot, out_grad, u_one, u_two, cosine, sine, inverse)


def span(part, rows):
    side = part[1]
    return slice(0, rows) if side is None else slice(side * rows // 2, (side + 1) * rows // 2)


def features(ref, part):
    return ref[part[0]][:, span(part, ref.shape[2])]


def both_vgs(vgs, vgs_t):
    return jnp.concatenate([vgs[...], vgs_t[...]], axis=0)


def pair(mine, theirs, part):
    return jnp.concatenate([features(mine, part), features(theirs, part)], axis=0)


def values_kernel(*refs, parts, first, last):
    mine, theirs = refs[0], refs[1]
    weights, rest = refs[2 : 2 + len(parts)], refs[2 + len(parts) :]
    tokens = mine.shape[1]
    acc = None
    if not first:
        acc, rest = rest[0][...], rest[1:]
    for part, w in zip(parts, weights, strict=True):
        product = mm(pair(mine, theirs, part), w[...], (1, 0))
        acc = product if acc is None else acc + product
    if not last:
        rest[0][...] = acc
        return
    vgs, vgs_t, inverse, u_mine, packed = rest
    vgs = both_vgs(vgs, vgs_t).astype(F32)
    wide = acc.shape[1]
    u_mine[...] = acc[:tokens]
    packed[:, :wide] = acc[tokens:]
    dot_m = jnp.sum(acc[:tokens] * vgs[:tokens], axis=1, keepdims=True)
    dot_t = jnp.sum(acc[tokens:] * vgs[tokens:], axis=1, keepdims=True)
    packed[:, wide : wide + HD] = jnp.broadcast_to(dot_m, (tokens, HD))
    packed[:, wide + HD : wide + 2 * HD] = jnp.broadcast_to(dot_t, (tokens, HD))
    packed[:, wide + 2 * HD :] = inverse[...]


def values_sum(mine, theirs, parts, weights, before=(), final=()):
    tokens, wide = mine.shape[1], weights[0].shape[1]
    if final:
        out = [sds((tokens, wide), F32), sds((tokens, wide + 3 * HD), F32)]
    else:
        out = sds((2 * tokens, wide), F32)
    return pl.pallas_call(
        functools.partial(values_kernel, parts=parts, first=not before, last=bool(final)),
        out_shape=out,
        compiler_params=params(),
        cost_estimate=SMALL,
        name="values",
    )(mine, theirs, *weights, *before, *final)


def first_kernel(*refs, count):
    vgs, vgs_t, gain = refs[:3]
    weights, (out_m, out_t) = refs[3 : 3 + count], refs[3 + count :]
    tokens = vgs.shape[0]
    left = both_vgs(vgs, vgs_t)
    for i in range(count):
        part = mm(left, weights[i][...], (1, 1)) * gain[i]
        out_m[i] = part[:tokens].astype(BF16)
        out_t[i] = part[tokens:].astype(BF16)


def first_terms(vgs, vgs_t, gain, weights):
    count = len(weights)
    out = sds((count, vgs.shape[0], weights[0].shape[0]), BF16)
    return pl.pallas_call(
        functools.partial(first_kernel, count=count),
        out_shape=[out, out],
        compiler_params=params(),
        cost_estimate=SMALL,
        name="first_terms",
    )(vgs, vgs_t, gain, *weights)


def local_kernel(*refs, parts, shares, width):
    mine, theirs, vgs, vgs_t, gain, inverse, own, got = refs[:8]
    weights, outs = refs[8 : 8 + len(parts)], refs[8 + len(parts) :]
    blocks = sum(shares, [])
    rows = mine.shape[2]
    tokens, wide = vgs.shape
    one, two, three = (slice(wide + i * HD, wide + (i + 1) * HD) for i in range(3))
    inv_m, inv_t = inverse[...], got[:, three]
    c_m = inv_m * inv_m * (own[:, one] + got[:, two]) / width
    c_t = inv_t * inv_t * (own[:, two] + got[:, one]) / width
    coarse = c_m.astype(BF16)
    fine = (c_m - coarse.astype(F32)).astype(BF16)
    lane = lax.broadcasted_iota(jnp.int32, c_m.shape, 1)
    outs[0][:, len(blocks) * rows :] = jnp.where(lane < HD // 2, coarse.astype(F32), fine.astype(F32)).astype(BF16)
    c_m = jnp.concatenate([c_m] * (rows // HD), axis=1)
    c_t = jnp.concatenate([c_t] * (rows // HD), axis=1)
    left = both_vgs(vgs, vgs_t)
    for part, w in zip(parts, weights, strict=True):
        r, at = part[0], span(part, rows)
        n = blocks.index(r)
        to = slice(n * rows + at.start, n * rows + at.stop)
        g = gain[r][:, at]
        over = 1.0 / g
        product = mm(left, w[...], (1, 1))
        h_m, h_t = features(mine, part).astype(F32), features(theirs, part).astype(F32)
        outs[0][:, to] = (product[:tokens] * g - h_m * over * c_m[:, at]).astype(BF16)
        outs[1][:, to] = (product[tokens:] * g - h_t * over * c_t[:, at]).astype(BF16)


def local_grads(mine, theirs, vgs, vgs_t, gain, inverse, own, got, shares, parts, weights, width):
    tokens, rows = mine.shape[1:]
    wide = sum(len(share) for share in shares) * rows
    out = [sds((tokens, wide + HD), BF16), sds((tokens, wide), BF16)]
    return pl.pallas_call(
        functools.partial(local_kernel, parts=parts, shares=shares, width=width),
        out_shape=out,
        compiler_params=params(),
        cost_estimate=SMALL,
        name="local_grad",
    )(mine, theirs, vgs, vgs_t, gain, inverse, own, got, *weights)


def weight_kernel(*refs, part):
    mine, theirs, vgs, vgs_t = refs[:4]
    out = refs[-1]
    total = mm(pair(mine, theirs, part), both_vgs(vgs, vgs_t), (0, 0))
    rows = total.shape[0]
    for side, arrived in enumerate(refs[4:-1]):
        if arrived is None:
            continue
        if arrived.shape[0] == rows:
            total = total + arrived[...].astype(F32)
        elif side == 0:
            total = jnp.concatenate([total[: rows // 2] + arrived[...].astype(F32), total[rows // 2 :]], axis=0)
        else:
            total = jnp.concatenate([total[: rows // 2], total[rows // 2 :] + arrived[...].astype(F32)], axis=0)
    out[...] = total.astype(BF16)


def weight_step(mine, theirs, vgs, vgs_t, part, from_behind=None, from_ahead=None):
    at = span(part, mine.shape[2])

    def kernel(*refs):
        refs = list(refs)
        if from_behind is None:
            refs.insert(4, None)
        if from_ahead is None:
            refs.insert(5, None)
        weight_kernel(*refs, part=part)

    arrived = [x for x in (from_behind, from_ahead) if x is not None]
    return pl.pallas_call(
        kernel,
        out_shape=sds((at.stop - at.start, vgs.shape[1]), BF16),
        compiler_params=params(),
        cost_estimate=SMALL,
        name="weight_step",
    )(mine, theirs, vgs, vgs_t, *arrived)


def weight_both_kernel(*refs, parts):
    mine, theirs, vgs, vgs_t = refs[:4]
    arrived, outs = refs[4:-2], refs[-2:]
    right = both_vgs(vgs, vgs_t)
    for i, (part, out) in enumerate(zip(parts, outs, strict=True)):
        total = mm(pair(mine, theirs, part), right, (0, 0))
        rows = total.shape[0]
        if arrived:
            more = arrived[i][...].astype(F32)
            if more.shape[0] == rows:
                total = total + more
            elif i == 0:
                total = jnp.concatenate([total[: rows // 2] + more, total[rows // 2 :]], axis=0)
            else:
                total = jnp.concatenate([total[: rows // 2], total[rows // 2 :] + more], axis=0)
        out[...] = total.astype(BF16)


def weight_both(mine, theirs, vgs, vgs_t, parts, arrived):
    ats = [span(part, mine.shape[2]) for part in parts]
    return pl.pallas_call(
        functools.partial(weight_both_kernel, parts=parts),
        out_shape=[sds((at.stop - at.start, vgs.shape[1]), BF16) for at in ats],
        compiler_params=params(),
        cost_estimate=SMALL,
        name="weight_both",
    )(mine, theirs, vgs, vgs_t, *arrived)


def weight_last_kernel(mine, theirs, vgs, vgs_t, f, b, out, held, sem):
    right = both_vgs(vgs, vgs_t)
    half = f.shape[0] // 2
    copies = []
    for side in range(2):
        at = slice(side * half, (side + 1) * half)
        total = mm(pair(mine, theirs, (0, side)), right, (0, 0))
        held[at, :] = (total + f[at, :].astype(F32) + b[at, :].astype(F32)).astype(BF16)
        copies.append(pltpu.make_async_copy(held.at[at, :], out.at[at, :], sem.at[side]))
        copies[-1].start()
    for copy in copies:
        copy.wait()


def weight_last(mine, theirs, vgs, vgs_t, f, b):
    return pl.pallas_call(
        weight_last_kernel,
        out_specs=pl.BlockSpec(memory_space=pl.ANY),
        out_shape=sds(f.shape, BF16),
        scratch_shapes=[pltpu.VMEM(f.shape, BF16), pltpu.SemaphoreType.DMA((2,))],
        compiler_params=params(),
        cost_estimate=SMALL,
        name="weight_last",
    )(mine, theirs, vgs, vgs_t, f, b)


def copies_of(pieces, shares, where, out, sem, first, rows):
    copies = []
    for piece, blocks in zip(pieces, shares, strict=True):
        for j, r in enumerate(blocks):
            column = pl.multiple_of(where[first + r] * rows, rows)
            source, target = piece.at[:, j * rows : (j + 1) * rows], out.at[:, pl.ds(column, rows)]
            copies.append(pltpu.make_async_copy(source, target, sem.at[len(copies)]))
    return copies


def early_kernel(where, pin, ones, twos, raw_m, raw_t, second, *refs, soon, shares, chips, rows):
    pieces, (out, done, sem, sems) = refs[:-4], refs[-4:]
    copies = copies_of(pieces, shares, where, out, sem, 1, rows)
    for copy in copies:
        copy.start()
    c = second[...].astype(F32)
    c = c + pltpu.roll(c, HD // 2, 1)
    c = jnp.concatenate([c] * (rows // HD), axis=1)
    for side, (terms, raw) in enumerate(((ones, raw_m), (twos, raw_t))):
        for i, r in enumerate(soon):
            done[side, i] = (terms[i].astype(F32) - raw[i].astype(F32) * c).astype(BF16)
            column = pl.multiple_of(where[1 + side * chips + r] * rows, rows)
            copies.append(pltpu.make_async_copy(done.at[side, i], out.at[:, pl.ds(column, rows)], sems.at[side, i]))
            copies[-1].start()
    for copy in copies:
        copy.wait()


def early_blocks(where, pin, ones, twos, raw_m, raw_t, pieces, soon, shares, chips, width):
    _, tokens, rows = ones.shape
    somewhere = pl.BlockSpec(memory_space=pl.ANY)
    return pl.pallas_call(
        functools.partial(early_kernel, soon=soon, shares=shares, chips=chips, rows=rows),
        grid=(1,),
        in_specs=[
            pl.BlockSpec(memory_space=pltpu.SMEM),
            somewhere,
            pl.BlockSpec(ones.shape, lambda i: (0, 0, 0)),
            pl.BlockSpec(twos.shape, lambda i: (0, 0, 0)),
            pl.BlockSpec(ones.shape, lambda i: (0, 0, 0)),
            pl.BlockSpec(ones.shape, lambda i: (0, 0, 0)),
            pl.BlockSpec((tokens, HD), lambda i: (0, len(shares[0]) * rows // HD)),
        ]
        + [somewhere] * len(pieces),
        out_specs=somewhere,
        out_shape=sds((tokens, width), BF16),
        scratch_shapes=[
            pltpu.VMEM((2, *ones.shape), BF16),
            pltpu.SemaphoreType.DMA((sum(len(x) for x in shares),)),
            pltpu.SemaphoreType.DMA((2, len(soon))),
        ],
        compiler_params=params(),
        cost_estimate=SMALL,
        name="early_blocks",
    )(where, pin, ones, twos, raw_m, raw_t, pieces[0], *pieces)


def join_kernel(where, base, *refs, shares, chips, rows):
    pieces, (out, sem) = refs[:-2], refs[-2:]
    copies = copies_of(pieces, shares, where, out, sem, 1 + chips, rows)
    for copy in copies:
        copy.start()
    for copy in copies:
        copy.wait()


def join(where, base, pieces, shares, chips, rows):
    somewhere = pl.BlockSpec(memory_space=pl.ANY)
    return pl.pallas_call(
        functools.partial(join_kernel, shares=shares, chips=chips, rows=rows),
        in_specs=[pl.BlockSpec(memory_space=pltpu.SMEM)] + [somewhere] * (1 + len(pieces)),
        out_specs=somewhere,
        out_shape=sds(base.shape, BF16),
        input_output_aliases={1: 0},
        scratch_shapes=[pltpu.SemaphoreType.DMA((sum(len(x) for x in shares),))],
        compiler_params=params(),
        cost_estimate=SMALL,
        name="join",
    )(where, base, *pieces)


def fence_kernel(x, out):
    out[...] = x[...]


def fence(x, us):
    return pl.pallas_call(
        fence_kernel,
        out_shape=sds(x.shape, x.dtype),
        compiler_params=params(),
        cost_estimate=cost(us),
        name="fence",
    )(x)


def last_layer(layer_counts, layers):
    sections, mine = lax.axis_size("section"), lax.axis_index("section")
    own = layer_counts[0]
    total = own
    if sections > 2:
        reach = 1
        while reach < sections:
            route = [(i, i + reach) for i in range(sections - reach)]
            total = total + lax.ppermute(total, "section", route)
            reach *= 2
    return jnp.where(mine == sections - 1, layers, total) - 1


def shards(hidden, gain_table, layer_counts, positions, queries, keys, value_weight, out_grad):
    tokens_in, weight = hidden[0], value_weight[0]
    tokens, width = tokens_in.shape
    rows = weight.shape[0]
    sections = lax.axis_size("section")
    devices = lax.axis_size("dp")
    chips = devices // 2
    ring = list(range(0, chips, 2)) + list(range(1, chips, 2))[::-1]
    place_of = [ring.index(c) for c in range(chips)]
    me = lax.axis_index("dp")
    chip, core = me // 2, me % 2
    place = jnp.where(chip % 2 == 0, chip // 2, chips - 1 - chip // 2)
    spots = (place + jnp.arange(chips, dtype=jnp.int32)) % chips
    order = 2 * jnp.where(spots < (chips + 1) // 2, 2 * spots, 2 * (chips - 1 - spots) + 1)

    def hop(d, by):
        return 2 * ring[(place_of[d // 2] + by) % chips] + d % 2

    forth = [(d, hop(d, 1)) for d in range(devices)]
    back = [(d, hop(d, -1)) for d in range(devices)]
    swap = [(d, d ^ 1) for d in range(devices)]
    down = [(s * devices + d, (s - 1) * devices + d) for s in range(1, sections) for d in range(devices)]
    cross = [(s * devices + d, (s - 1) * devices + (d ^ 1)) for s in range(1, sections) for d in range(devices)]

    half = chips // 2
    low, high = slice(0, rows // 2), slice(rows // 2, rows)
    soon = [0, 1, chips - 1]
    later = [[r for r in range(chips) if r not in soon]]

    def ahead(x):
        return lax.ppermute(x, "dp", forth)

    def behind(x):
        return lax.ppermute(x, "dp", back)

    def swapped(x):
        return lax.ppermute(x, "dp", swap)

    def sent_down(x):
        return lax.ppermute(x, ("section", "dp"), down)

    def sent_across(x):
        return lax.ppermute(x, ("section", "dp"), cross)

    token = []

    def after(x):
        x = lax.optimization_barrier((x, *token))[0] if token else x
        token[:] = [x]
        return x

    def then(*results):
        token[:] = [results[0]]
        return results if len(results) > 1 else results[0]

    pin = [jnp.zeros((8, HD), F32)]

    def hold(us):
        pin[0] = then(fence(after(pin[0]), us))

    def parts_of(some):
        return [part for part in held if part[0] in some]

    def weights(parts):
        return [held[part] for part in parts]

    held = {(0, None): weight}
    moving = {(chips - 1, None): ahead(weight), (1, None): behind(weight)}

    def gather_next(step, side):
        for r, back_r, half_side, move in ((chips - step, chips - step + 1, side, ahead), (step, step - 1, 1 - side, behind)):
            if step == 2:
                source = held[back_r, None][high if half_side else low]
            else:
                source = held[back_r, half_side]
            moving[r, half_side] = move(source)

    def gather_here(step, side):
        for key in ((chips - step, side), (step, 1 - side)):
            held[key] = after(moving.pop(key))

    last = last_layer(layer_counts, gain_table.shape[0])
    where = jnp.concatenate([last[None], order + core, order + 1 - core]).astype(jnp.int32)
    cosine, sine = rope_tables(positions[0])
    raw_m, raw_t = then(*pick(where, tokens_in, soon, chips, rows))
    raw_m = sent_down(raw_m)
    mine, send, gain, inverse = then(*prep(after(where), tokens_in, gain_table, chips, rows))
    theirs = swapped(send)
    probs, q_rot, k_rot, vgs = then(
        *attention_probs(queries[0], keys[0], out_grad[0], cosine, sine, after(inverse))
    )
    vgs_t = swapped(vgs)
    hold(H[0])
    for key in ((chips - 1, None), (1, None)):
        held[key] = after(moving.pop(key))
    gather_next(2, 0)
    theirs, vgs_t = after(theirs), after(vgs_t)
    soon_gain = jnp.concatenate([gain[r : r + 1] for r in soon], axis=0)
    parts = parts_of(soon)
    one, two = then(*first_terms(after(vgs), vgs_t, soon_gain, [held[r, None] for r in soon]))
    late = {r: after(held[r, None]) for r in (chips - 1, 1)}
    moving[chips - 2, 1] = ahead(late[chips - 1][high])
    moving[2, 0] = behind(late[1][low])
    raw_m = after(raw_m)
    one = sent_down(after(one))
    total = then(values_sum(after(mine), theirs, parts, weights(parts)))
    hold(H[1])
    for step in range(2, half):
        gather_here(step, 0)
        if step + 1 <= half:
            gather_next(step + 1, 0)
        hold(H[2])
        gather_here(step, 1)
        if step + 1 < half:
            gather_next(step + 1, 1)
        if step == 2:
            one = after(one)
            two = sent_across(after(two))
        if step < half - 1:
            parts = parts_of([step, chips - step])
            total = then(values_sum(after(mine), theirs, parts, weights(parts), (total,)))
            hold(H[3])

    def weight_parts(parts, *arrived):
        arrived = [after(x) for x in arrived]
        f, b = then(*weight_both(after(mine), theirs, vgs, vgs_t, parts, arrived))
        return ahead(f), behind(b)

    f, b = weight_parts(((half, 0), (half, 1)))
    two = after(two)
    raw_t = sent_down(after(raw_t))
    hold(H[4])
    parts = parts_of([half - 1, half + 1])
    total = then(values_sum(after(mine), theirs, parts, weights(parts), (total,)))
    for key in ((half, 0), (half, 1)):
        held[key] = after(moving.pop(key))
    parts = parts_of([half])
    u_mine, packed = values_sum(after(mine), theirs, parts, weights(parts), (total,), (vgs, vgs_t, inverse))
    got = swapped(then(packed))

    def weight_part(part, *arrived):
        return then(weight_step(after(mine), theirs, vgs, vgs_t, part, *arrived))

    def weight_turn(r, f, b):
        f = ahead(weight_part((r, None), after(f)))
        b = behind(weight_part((chips - r, None), None, after(b)))
        return f, b

    if half > 2:
        f, b = weight_parts(((half - 1, None), (half + 1, None)), f, b)
    hold(H[5])
    got = after(got)
    parts = parts_of(sum(later, []))
    m, t = then(
        *local_grads(
            mine, theirs, after(vgs), vgs_t, gain, inverse, packed, got, later, parts, weights(parts), width
        )
    )
    m, t = sent_down(m), sent_across(t)
    query_grad, key_grad = then(
        *attention_back(probs, q_rot, k_rot, out_grad[0], after(u_mine), got, cosine, sine, inverse)
    )
    hold(H[6])
    for r in range(half - 2, 0, -1):
        f, b = weight_turn(r, f, b)
        if r == 2:
            raw_t = after(raw_t)
        hold(H[7])
    upstream = then(
        early_blocks(where, pin[0], one, two, raw_m, raw_t, [after(m)], soon, [sum(later, [])], chips, width)
    )
    t = after(t)
    upstream = then(join(where, after(upstream), [t], [sum(later, [])], chips, rows))
    f, b = after(f), after(b)
    weight_grad = weight_last(mine, theirs, vgs, vgs_t, f, b)
    return (query_grad[None], key_grad[None], weight_grad[None], upstream[None])


def solution(mesh):
    split = P("section", "dp", None)
    in_specs = (split, P(), P("section"), P("section", "dp"), split, split, split, split)
    out_specs = (split,) * 4
    return jax.shard_map(shards, mesh=mesh, in_specs=in_specs, out_specs=out_specs, check_vma=False)
```
